256 devices in a mesh: tm: 8 (over y, z_lo), tp: 32 (over z_hi, x, core).
Axes of the slice: x: 4, y: 4, z: 8 (z_hi: 4, z_lo: 2; z = z_hi * 2 + z_lo), core: 2. Of those that a mesh axis runs over, the one named last changes fastest.
Arguments:
- features: bfloat16 [8, 64, 30, 512], P('tm', None, None, 'tp'), may hold values from -6 to 6
- weight_one: bfloat16 [3, 3, 3, 512, 512], P(None, None, None, None, 'tp'), may hold values from -0.0546875 to 0.0546875
- weight_two: bfloat16 [3, 3, 3, 512, 256], replicated, may hold values from -0.0546875 to 0.0546875
- weight_three: bfloat16 [3, 3, 3, 256, 256], replicated, may hold values from -0.078125 to 0.078125
Outputs:
- decoded: bfloat16 [8, 128, 60, 256], P('tm', 'tp')
The draws below stay inside these ranges and needn't reach their ends.
All inputs are finite; a program needn't handle non-finite values.
Results may differ from the reference program's by a relative error of at most 0.019.
Values may be sent and summed in bfloat16 or wider, within the bound.
No kernel may reach another device: no remote copies, remote signals or barrier semaphores. Data moves between devices by JAX's collectives and lax.ppermute only.
A program may use at most 128 MiB of HBM per device.

```python
import jax
import jax.numpy as jnp
from jax import lax

C1 = 512
C2 = 256
W1 = 30
H1 = 64
FRAMES = 8


def levels(own_key, shape, shards, low, high):
    gain, own = 1.0, jax.random.fold_in(own_key, 6)
    for axis_at, shards_of in shards:
        heights = jnp.exp(jax.random.uniform(jax.random.fold_in(own, axis_at), (shards_of,), jnp.float32, low / len(shards), high / len(shards)))
        gain = gain * jnp.repeat(heights, shape[axis_at] // shards_of).reshape([-1 if axis == axis_at else 1 for axis in range(len(shape))])
    return gain


def noise(rng, dims, deviation, bound, shards=(), kind=jnp.bfloat16):
    gain = levels(rng, dims, shards, -0.22, 0.18) if shards else 1.0
    values = jax.random.normal(rng, dims, jnp.float32) * deviation * gain
    return jnp.minimum(jnp.maximum(values, -bound), bound).astype(kind)


def setup_inputs(seed: int = 0) -> dict:
    key_of = jax.random.split(jax.random.key(seed), 5)
    features = noise(key_of[0], (FRAMES, H1, W1, C1), 1.0, 6.0, ((0, 8), (3, 32)))
    weight_one = noise(key_of[1], (3, 3, 3, C1, C1), (27 * C1) ** -0.5, 0.0546875, ((4, 32),))
    weight_two = noise(key_of[2], (3, 3, 3, C1, C2), (27 * C1) ** -0.5, 0.0546875)
    weight_three = noise(key_of[3], (3, 3, 3, C2, C2), (27 * C2) ** -0.5, 0.078125)
    return dict(features=features, weight_one=weight_one, weight_two=weight_two, weight_three=weight_three)


def silu_round(values):
    return jax.nn.silu(values.astype(jnp.float32)).astype(jnp.bfloat16)


def causal_conv(field, kernel):
    values = field.astype(jnp.float32)
    extended = jnp.concatenate([values[:1], values[:1], values], axis=0)[None]
    result = lax.conv_general_dilated(extended, kernel.astype(jnp.float32), (1, 1, 1), ((0, 0), (1, 1), (1, 1)), dimension_numbers=("NDHWC", "DHWIO", "NDHWC"), precision=lax.Precision.HIGHEST)
    return result[0]


def reference(features, weight_one, weight_two, weight_three):
    act_in = silu_round(features)
    level_one = (features.astype(jnp.float32) + causal_conv(act_in, weight_one)).astype(jnp.bfloat16)
    act_mid = silu_round(level_one)
    upsampled = jnp.repeat(jnp.repeat(act_mid, 2, axis=1), 2, axis=2)
    block_mid = causal_conv(upsampled, weight_two).astype(jnp.bfloat16)
    act_out = silu_round(block_mid)
    return (block_mid.astype(jnp.float32) + causal_conv(act_out, weight_three)).astype(jnp.bfloat16)
```

```python
import functools

import jax
import jax.numpy as jnp
from jax import lax
from jax.experimental import pallas as pl
from jax.experimental.pallas import tpu as pltpu
from jax.sharding import Mesh, PartitionSpec as P

PITCH = 32
EDGE = 128
BF16 = jnp.bfloat16
F32 = jnp.float32
SMEM = pl.BlockSpec(memory_space=pltpu.SMEM)
VMEM = pl.BlockSpec(memory_space=pltpu.VMEM)
LIMIT = 48 * 2**20


def call(kernel, out_shape, operands, scratch=()):
    specs = [SMEM] + [VMEM] * (len(operands) - 1)
    return pl.pallas_call(
        kernel,
        out_shape=out_shape,
        in_specs=specs,
        out_specs=jax.tree.map(lambda _: VMEM, out_shape),
        scratch_shapes=scratch,
        compiler_params=pltpu.CompilerParams(vmem_limit_bytes=LIMIT),
    )(*operands)


def silu(v):
    return v / (1.0 + jnp.exp(-v))


def column_mask(shape, axis, across):
    return lax.rem(lax.broadcasted_iota(jnp.int32, shape, axis), PITCH) < across


def coarse_kernel(height, at_ref, field_ref, weight_ref, *refs):
    blocks, (first_ref, second_ref, own_ref, all_ref, prod_ref) = refs[:8], refs[8:]
    shard = field_ref.shape[0]
    cells = height * PITCH
    z, x, c, t = at_ref[0], at_ref[1], at_ref[2], at_ref[3]
    for n, block in enumerate(blocks):
        x_from = lax.rem(x + 4 - n // 2, 4)
        c_from = c if n % 2 == 0 else 1 - c
        for p in range(4):
            z_from = lax.rem(z + 4 - p, 4)
            base = pl.multiple_of(((z_from * 4 + x_from) * 2 + c_from) * shard, shard)
            all_ref[pl.ds(base, shard), :] = block[p * shard : (p + 1) * shard, :]
    rows = prod_ref.shape[0]
    prod_ref[:, :EDGE] = jnp.zeros((rows, EDGE), F32)
    prod_ref[:, EDGE + cells :] = jnp.zeros((rows, EDGE), F32)
    span = 512
    for n in range(cells // span):
        prod_ref[:, EDGE + n * span : EDGE + (n + 1) * span] = jnp.dot(
            weight_ref[...], all_ref[:, n * span : (n + 1) * span], preferred_element_type=F32
        )
    start = t == 0
    span = 512
    for n in range(cells // span):
        lo = n * span
        sums = []
        for k in range(3):
            total = None
            for i in range(3):
                for j in range(3):
                    tap = (k * 3 + i) * 3 + j
                    off = (i - 1) * PITCH + j - 1
                    wide = prod_ref[tap * shard : (tap + 1) * shard, lo : lo + span + 2 * EDGE]
                    if off != 0:
                        wide = pltpu.roll(wide, (-off) % (span + 2 * EDGE), 1)
                    piece = wide[:, EDGE : EDGE + span]
                    total = piece if total is None else total + piece
            sums.append(total)
        late = sums[0] + sums[1]
        first_ref[:, lo : lo + span] = jnp.where(start, late, sums[1]).astype(BF16)
        second_ref[:, lo : lo + span] = sums[0].astype(BF16)
        own = field_ref[:, lo : lo + span].astype(F32) + sums[2]
        own_ref[:, lo : lo + span] = jnp.where(start, own + late, own)


def strips_kernel(height, across, at_ref, own_ref, first_ref, second_ref, out_ref, wide_ref):
    t = at_ref[3]
    cells = height * PITCH
    shard = own_ref.shape[0]
    wide_ref[:, :EDGE] = jnp.zeros((shard, EDGE), F32)
    wide_ref[:, EDGE + cells :] = jnp.zeros((shard, EDGE), F32)
    zero = jnp.zeros((shard, cells), F32)
    level = (
        own_ref[...]
        + jnp.where(t >= 1, first_ref[...].astype(F32), zero)
        + jnp.where(t >= 2, second_ref[...].astype(F32), zero)
    )
    act = silu(level.astype(BF16).astype(F32))
    wide_ref[:, EDGE : EDGE + cells] = jnp.where(column_mask(act.shape, 1, across), act, 0.0)
    for s in range(height // 2):
        lo = EDGE + 2 * s * PITCH - PITCH
        base = lo // 128 * 128
        piece = pltpu.roll(wide_ref[:, base : base + 256], 256 - (lo - base), 1)[:, :128]
        out_ref[s] = piece.astype(BF16)


def down(v):
    return pltpu.roll(v, 1, 0)


def up(v):
    return pltpu.roll(v, v.shape[0] - 1, 0)


def fine_kernel(across, at_ref, a0_ref, a1_ref, a2_ref, wide_ref, last_ref, first_ref, second_ref, own_ref):
    t, strip, strips = at_ref[3], at_ref[4], at_ref[5]
    frames = []
    a0 = a0_ref[...].astype(F32)
    a1 = jnp.where(t >= 1, a1_ref[...].astype(F32), a0)
    a2 = jnp.where(t >= 2, a2_ref[...].astype(F32), a1)
    for a in (a2, a1, a0):
        frames.append(a.T.astype(BF16))
    spans = ((0, 3), (0, 4), (1, 4))
    maps = ((0, 0, 1, 1, 2, 2), (0, 1, 1, 2, 2, 3), (0, 0, 1, 1, 2, 2))
    even, odd = [None] * 6, [None] * 6
    for i in range(3):
        lo, hi = spans[i]
        sums = []
        for j in range(3):
            total = None
            for k in range(3):
                part = jnp.dot(frames[k][lo * PITCH : hi * PITCH], wide_ref[k, i, j], preferred_element_type=F32)
                total = part if total is None else total + part
            sums.append(total)
        at_even = down(sums[0]) + sums[1] + sums[2]
        at_odd = sums[0] + sums[1] + up(sums[2])
        for r in range(6):
            at = slice(maps[i][r] * PITCH, (maps[i][r] + 1) * PITCH)
            even[r] = at_even[at] if even[r] is None else even[r] + at_even[at]
            odd[r] = at_odd[at] if odd[r] is None else odd[r] + at_odd[at]
    mid = [jnp.concatenate(rows, 0).astype(BF16).astype(F32) for rows in (even, odd)]
    shape = mid[0].shape
    row = lax.broadcasted_iota(jnp.int32, shape, 0) // PITCH
    keep = column_mask(shape, 0, across)
    keep = keep & ((row > 0) | (strip > 0)) & ((row < 5) | (strip < strips - 1))
    acts = [jnp.where(keep, silu(m), 0.0).astype(BF16) for m in mid]
    size = 4 * PITCH
    sums = []
    for k in range(3):
        parts = []
        for j in range(3):
            total = None
            for i in range(3):
                rows = slice(i * PITCH, i * PITCH + size)
                both = jnp.concatenate([acts[0][rows], acts[1][rows]], 0)
                part = jnp.dot(both, last_ref[k, i, j], preferred_element_type=F32)
                total = part if total is None else total + part
            parts.append(total)
        at_even = down(parts[0][size:]) + parts[1][:size] + parts[2][size:]
        at_odd = parts[0][:size] + parts[1][size:] + up(parts[2][:size])
        sums.append(jnp.concatenate([at_even, at_odd], 0))
    start = t == 0
    late = sums[0] + sums[1]
    first_ref[...] = jnp.where(start, late, sums[1]).astype(BF16)
    second_ref[...] = sums[0].astype(BF16)
    rows = slice(PITCH, PITCH + size)
    own = jnp.concatenate([mid[0][rows], mid[1][rows]], 0) + sums[2]
    own_ref[...] = jnp.where(start, own + late, own)


def last_kernel(across, at_ref, own_ref, first_ref, second_ref, out_ref, order_ref):
    t = at_ref[3]
    zero = jnp.zeros(own_ref.shape, F32)
    total = (
        own_ref[...]
        + jnp.where(t >= 1, first_ref[...].astype(F32), zero)
        + jnp.where(t >= 2, second_ref[...].astype(F32), zero)
    )
    for parity in range(2):
        for h in range(4):
            at = (parity * 4 + h) * PITCH
            for half in range(2):
                order_ref[half, pl.ds(4 * parity + h, PITCH, stride=8), :] = total[
                    at : at + PITCH, 128 * half : 128 * half + 128
                ]
    for half in range(2):
        out_ref[:, 128 * half : 128 * half + 128] = order_ref[half, : 4 * across * 2].astype(BF16)


def turned(block, axis, distance):
    count = lax.axis_size(axis)
    return lax.ppermute(block, axis, [(i, (i + distance) % count) for i in range(count)])


def on_device(features, weight_one, weight_two, weight_three):
    own_block = features[0]
    height, across, shard = own_block.shape
    channels = weight_one.shape[3]
    cells = height * PITCH
    tp = ("z", "x", "c")
    at = jnp.stack(
        [lax.axis_index(a) for a in ("z", "x", "c", "tm")] + [lax.axis_index(tp), lax.axis_size(tp)]
    ).astype(jnp.int32)
    field = jnp.pad(jnp.transpose(own_block, (2, 0, 1)), ((0, 0), (0, 0), (0, PITCH - across))).reshape(shard, cells)
    act_in = silu(field.astype(F32)).astype(BF16)
    column = jnp.concatenate([act_in] + [turned(act_in, "z", d) for d in (1, 2, 3)], 0)
    blocks = []
    for d in range(4):
        block = turned(column, "x", d) if d else column
        blocks += [block, turned(block, "c", 1)]
    kernel = jnp.transpose(weight_one, (0, 1, 2, 4, 3)).reshape(27 * shard, channels)
    small = jax.ShapeDtypeStruct((shard, cells), BF16)
    first, second, own = call(
        functools.partial(coarse_kernel, height),
        (small, small, jax.ShapeDtypeStruct((shard, cells), F32)),
        (at, field, kernel, *blocks),
        (pltpu.VMEM((channels, cells), BF16), pltpu.VMEM((27 * shard, cells + 2 * EDGE), F32)),
    )
    strips = lax.axis_size(tp)
    cut = call(
        functools.partial(strips_kernel, height, across),
        jax.ShapeDtypeStruct((strips, shard, 4 * PITCH), BF16),
        (at, own, turned(first, "tm", 1), turned(second, "tm", 2)),
        (pltpu.VMEM((shard, cells + 2 * EDGE), F32),),
    )
    strip = lax.all_to_all(cut, tp, 0, 0, tiled=True).reshape(channels, 4 * PITCH)
    width = weight_two.shape[4]
    small = jax.ShapeDtypeStruct((8 * PITCH, width), BF16)
    first, second, own = call(
        functools.partial(fine_kernel, across),
        (small, small, jax.ShapeDtypeStruct((8 * PITCH, width), F32)),
        (at, strip, turned(strip, "tm", 1), turned(strip, "tm", 2), weight_two, weight_three),
    )
    decoded = call(
        functools.partial(last_kernel, across),
        jax.ShapeDtypeStruct((8 * across, width), BF16),
        (at, own, turned(first, "tm", 1), turned(second, "tm", 2)),
        (pltpu.VMEM((2, 8 * PITCH, 128), F32),),
    )
    return jnp.transpose(decoded.reshape(2 * across, 4, width), (1, 0, 2))[None]


def solution(mesh):
    grid = Mesh(mesh.devices.reshape(mesh.shape["tm"], 4, 4, 2), ("tm", "z", "x", "c"))
    tp = ("z", "x", "c")
    return jax.shard_map(
        on_device,
        mesh=grid,
        in_specs=(P("tm", None, None, tp), P(None, None, None, None, tp), P(), P()),
        out_specs=P("tm", tp, None, None),
        check_vma=False,
    )
```

```python
import functools

import jax
import jax.numpy as jnp
from jax import lax
from jax.experimental import pallas as pl
from jax.experimental.pallas import tpu as pltpu
from jax.sharding import Mesh, PartitionSpec as P

PITCH = 32
LANES = 128
QUARTERS = 4
BF16 = jnp.bfloat16
F32 = jnp.float32
SMEM = pl.BlockSpec(memory_space=pltpu.SMEM)
ANY = pl.BlockSpec(memory_space=pl.ANY)
VMEM = pl.BlockSpec(memory_space=pltpu.VMEM)
LIMIT = 20 * 2**20


def call(kernel, out_shape, operands, scratch=(), specs=None):
    specs = specs or [SMEM] + [VMEM] * (len(operands) - 1)
    return pl.pallas_call(
        kernel,
        out_shape=out_shape,
        in_specs=specs,
        out_specs=jax.tree.map(lambda _: VMEM, out_shape),
        scratch_shapes=scratch,
        compiler_params=pltpu.CompilerParams(vmem_limit_bytes=LIMIT),
    )(*operands)


def silu(v):
    return v / (1.0 + jnp.exp(-v))


def column_mask(shape, axis, across):
    return lax.rem(lax.broadcasted_iota(jnp.int32, shape, axis), PITCH) < across


def before(block):
    lane = lax.broadcasted_iota(jnp.int32, block.shape, 1)
    return jnp.where(lane >= PITCH, pltpu.roll(block, PITCH, 1), 0.0)


def after(block):
    lane = lax.broadcasted_iota(jnp.int32, block.shape, 1)
    return jnp.where(lane < LANES - PITCH, pltpu.roll(block, LANES - PITCH, 1), 0.0)


def pack_kernel(field_ref, weight_ref, packed_ref, act_ref, slices_ref, raw_ref, columns_ref, rows_ref, sems):
    across, shard, height = field_ref.shape
    deep = height // QUARTERS
    load = pltpu.make_async_copy(field_ref, raw_ref, sems.at[4])
    load.start()
    width = weight_ref.shape[1] // 4
    copies = []
    for d in range(4):
        source = weight_ref.at[:, d * width : (d + 1) * width]
        copies.append(pltpu.make_async_copy(source, slices_ref.at[d], sems.at[d]))
        copies[d].start()
    columns_ref[...] = jnp.zeros(columns_ref.shape, F32)
    load.wait()
    columns_ref[: across * shard, :height] = raw_ref[...].astype(F32).reshape(across * shard, height)
    for c in range(shard):
        cells = columns_ref[pl.ds(c, PITCH, stride=shard), :].T
        quarters = [cells[q * deep : (q + 1) * deep] for q in range(QUARTERS)]
        rows_ref[pl.ds(c, deep, stride=shard), :] = jnp.concatenate(quarters, 1)
    for v in range(deep):
        values = rows_ref[v * shard : (v + 1) * shard, :]
        packed_ref[:, v * LANES : (v + 1) * LANES] = values.astype(BF16)
        act_ref[:, v * LANES : (v + 1) * LANES] = silu(values).astype(BF16)
    for copy in copies:
        copy.wait()


def coarse_kernel(at_ref, field_ref, slices_ref, *refs):
    blocks, (out_ref, all_ref, taps_ref, sum_ref) = refs[:8], refs[8:]
    shard, cells = field_ref.shape
    deep = cells // LANES
    group = 8 * shard
    wide = 4 * shard
    z, x, c, t = at_ref[0], at_ref[1], at_ref[2], at_ref[3]
    for n, block in enumerate(blocks):
        x_from = lax.rem(x + 4 - n // 2, 4)
        c_from = c if n % 2 == 0 else 1 - c
        base = (x_from * 2 + c_from) * shard
        for k in range(3):
            part = pl.multiple_of(jnp.minimum(t, 2 - k) * shard, shard)
            all_ref[pl.ds(pl.multiple_of(k * group + base, shard), shard), LANES : LANES + cells] = block[
                pl.ds(part, shard), :
            ]
    first, last = all_ref[:, LANES : 2 * LANES], all_ref[:, cells : cells + LANES]
    all_ref[:, :LANES] = before(last.astype(F32)).astype(BF16)
    all_ref[:, LANES + cells :] = after(first.astype(F32)).astype(BF16)
    for d in range(4):
        for k in range(3):
            for i in range(3):
                for j in range(3):
                    tap = (k * 3 + i) * 3 + j
                    to = j * wide + d * shard
                    taps_ref[i, to : to + shard, k * group : (k + 1) * group] = slices_ref[
                        d, tap * shard : (tap + 1) * shard, :
                    ]
    span = 4 * LANES
    for n in range(cells // span):
        total = None
        for i in range(3):
            lo = i * LANES + n * span
            part = jnp.dot(taps_ref[i], all_ref[:, lo : lo + span], preferred_element_type=F32)
            total = part if total is None else total + part
        for v in range(4):
            left, here, right = (total[j * wide : (j + 1) * wide, v * LANES : (v + 1) * LANES] for j in range(3))
            lo = LANES + n * span + v * LANES
            sum_ref[:, lo : lo + LANES] = pltpu.roll(left, 1, 1) + here + pltpu.roll(right, LANES - 1, 1)
    own = pl.ds(pl.multiple_of(z * shard, shard), shard)
    sum_ref[own, LANES : LANES + cells] = sum_ref[own, LANES : LANES + cells] + field_ref[...].astype(F32)
    sum_ref[:, :LANES] = before(sum_ref[:, cells : cells + LANES])
    sum_ref[:, LANES + cells :] = after(sum_ref[:, LANES : 2 * LANES])
    at = lax.broadcasted_iota(jnp.int32, (wide, LANES), 1) // PITCH
    for m in range(deep // 2):
        rows = [sum_ref[:, (2 * m + r) * LANES : (2 * m + r + 1) * LANES] for r in range(4)]
        for q in range(QUARTERS):
            moved = [pltpu.roll(rows[r], (r - q) % 4 * PITCH, 1) if r != q else rows[r] for r in range(4)]
            strip = jnp.where(at < 2, jnp.where(at < 1, moved[0], moved[1]), jnp.where(at < 3, moved[2], moved[3]))
            out_ref[q * (deep // 2) + m] = strip.astype(BF16)


def strip_kernel(across, parts_ref, out_ref, order_ref):
    shard = parts_ref.shape[1] // 4
    for n in range(8):
        total = None
        for z in range(4):
            part = parts_ref[z * 8 + n].astype(F32)
            total = part if total is None else total + part
        act = silu(total.astype(BF16).astype(F32))
        act = jnp.where(column_mask(act.shape, 1, across), act, 0.0)
        for z in range(4):
            order_ref[(z * 8 + n) * shard : (z * 8 + n + 1) * shard, :] = act[z * shard : (z + 1) * shard]
    out_ref[...] = order_ref[...].T.astype(BF16)


def down(v):
    return pltpu.roll(v, 1, 0)


def up(v):
    return pltpu.roll(v, v.shape[0] - 1, 0)


def fine_kernel(across, at_ref, a0_ref, a1_ref, a2_ref, wide_ref, last_ref, first_ref, second_ref, own_ref):
    t, strip, strips = at_ref[3], at_ref[4], at_ref[5]
    a0 = a0_ref[...].astype(F32)
    a1 = jnp.where(t >= 1, a1_ref[...].astype(F32), a0)
    a2 = jnp.where(t >= 2, a2_ref[...].astype(F32), a1)
    frames = jnp.concatenate([a2, a1, a0], 1).astype(BF16)
    spans = ((0, 3), (0, 4), (1, 4))
    maps = ((0, 0, 1, 1, 2, 2), (0, 1, 1, 2, 2, 3), (0, 0, 1, 1, 2, 2))
    even, odd = [None] * 6, [None] * 6
    for i in range(3):
        lo, hi = spans[i]
        sums = []
        for j in range(3):
            sums.append(
                jnp.dot(frames[lo * PITCH : hi * PITCH], wide_ref[i * 3 + j], preferred_element_type=F32)
            )
        at_even = down(sums[0]) + sums[1] + sums[2]
        at_odd = sums[0] + sums[1] + up(sums[2])
        for r in range(6):
            at = slice(maps[i][r] * PITCH, (maps[i][r] + 1) * PITCH)
            even[r] = at_even[at] if even[r] is None else even[r] + at_even[at]
            odd[r] = at_odd[at] if odd[r] is None else odd[r] + at_odd[at]
    mid = [jnp.concatenate(rows, 0).astype(BF16).astype(F32) for rows in (even, odd)]
    shape = mid[0].shape
    row = lax.broadcasted_iota(jnp.int32, shape, 0) // PITCH
    keep = column_mask(shape, 0, across)
    keep = keep & ((row > 0) | (strip > 0)) & ((row < 5) | (strip < strips - 1))
    acts = [jnp.where(keep, silu(m), 0.0).astype(BF16) for m in mid]
    size = 4 * PITCH
    sums = []
    for k in range(3):
        parts = []
        for j in range(3):
            total = None
            for i in range(3):
                rows = slice(i * PITCH, i * PITCH + size)
                both = jnp.concatenate([acts[0][rows], acts[1][rows]], 0)
                part = jnp.dot(both, last_ref[k, i, j], preferred_element_type=F32)
                total = part if total is None else total + part
            parts.append(total)
        at_even = down(parts[0][size:]) + parts[1][:size] + parts[2][size:]
        at_odd = parts[0][:size] + parts[1][size:] + up(parts[2][:size])
        sums.append(jnp.concatenate([at_even, at_odd], 0))
    start = t == 0
    late = sums[0] + sums[1]
    first_ref[...] = jnp.where(start, late, sums[1]).astype(BF16)
    second_ref[...] = sums[0].astype(BF16)
    rows = slice(PITCH, PITCH + size)
    own = jnp.concatenate([mid[0][rows], mid[1][rows]], 0) + sums[2]
    own_ref[...] = jnp.where(start, own + late, own)


def last_kernel(across, at_ref, own_ref, first_ref, second_ref, out_ref, order_ref):
    t = at_ref[3]
    zero = jnp.zeros(own_ref.shape, F32)
    total = (
        own_ref[...]
        + jnp.where(t >= 1, first_ref[...].astype(F32), zero)
        + jnp.where(t >= 2, second_ref[...].astype(F32), zero)
    )
    for parity in range(2):
        for h in range(4):
            at = (parity * 4 + h) * PITCH
            for half in range(2):
                order_ref[half, pl.ds(4 * parity + h, PITCH, stride=8), :] = total[
                    at : at + PITCH, 128 * half : 128 * half + 128
                ]
    for half in range(2):
        out_ref[:, 128 * half : 128 * half + 128] = order_ref[half, : 4 * across * 2].astype(BF16)


def turned(block, axis, distance):
    count = lax.axis_size(axis)
    return lax.ppermute(block, axis, [(i, (i + distance) % count) for i in range(count)])


def on_device(features, weight_one, weight_two, weight_three):
    own_block = features[0]
    height, across, shard = own_block.shape
    channels = weight_one.shape[3]
    cells = height * PITCH
    tp = ("z", "x", "c")
    at = jnp.stack(
        [lax.axis_index(a) for a in ("z", "x", "c", "tm")] + [lax.axis_index(tp), lax.axis_size(tp)]
    ).astype(jnp.int32)
    kernel = jnp.transpose(weight_one, (0, 1, 2, 4, 3)).reshape(27 * shard, channels)
    small = jax.ShapeDtypeStruct((shard, cells), BF16)
    field, act_in, slices = call(
        pack_kernel,
        (small, small, jax.ShapeDtypeStruct((4, 27 * shard, channels // 4), BF16)),
        (jnp.transpose(own_block, (1, 2, 0)), kernel),
        (
            pltpu.VMEM((across, shard, height), BF16),
            pltpu.VMEM((PITCH * shard, LANES), F32),
            pltpu.VMEM((cells // LANES * shard, LANES), F32),
            pltpu.SemaphoreType.DMA((5,)),
        ),
        [ANY, ANY],
    )
    frames = jnp.concatenate([act_in, turned(act_in, "tm", 1), turned(act_in, "tm", 2)], 0)
    slices = lax.all_to_all(slices, "z", 0, 0, tiled=True)
    blocks = []
    for d in range(4):
        block = turned(frames, "x", d) if d else frames
        blocks += [block, turned(block, "c", 1)]
    strips = lax.axis_size(tp)
    cut = call(
        coarse_kernel,
        jax.ShapeDtypeStruct((strips, 4 * shard, LANES), BF16),
        (at, field, slices, *blocks),
        (
            pltpu.VMEM((3 * channels // 4, cells + 2 * LANES), BF16),
            pltpu.VMEM((3, 12 * shard, 3 * channels // 4), BF16),
            pltpu.VMEM((4 * shard, cells + 2 * LANES), F32),
        ),
    )
    parts = lax.all_to_all(cut, tp, 0, 0, tiled=True)
    strip = pl.pallas_call(
        functools.partial(strip_kernel, across),
        out_shape=jax.ShapeDtypeStruct((LANES, channels), BF16),
        scratch_shapes=[pltpu.VMEM((channels, LANES), F32)],
        compiler_params=pltpu.CompilerParams(vmem_limit_bytes=LIMIT),
    )(parts)
    width = weight_two.shape[4]
    wide = jnp.transpose(weight_two, (1, 2, 0, 3, 4)).reshape(9, 3 * channels, width)
    small = jax.ShapeDtypeStruct((8 * PITCH, width), BF16)
    first, second, own = call(
        functools.partial(fine_kernel, across),
        (small, small, jax.ShapeDtypeStruct((8 * PITCH, width), F32)),
        (at, strip, turned(strip, "tm", 1), turned(strip, "tm", 2), wide, weight_three),
    )
    decoded = call(
        functools.partial(last_kernel, across),
        jax.ShapeDtypeStruct((8 * across, width), BF16),
        (at, own, turned(first, "tm", 1), turned(second, "tm", 2)),
        (pltpu.VMEM((2, 8 * PITCH, 128), F32),),
    )
    return jnp.transpose(decoded.reshape(2 * across, 4, width), (1, 0, 2))[None]


def solution(mesh):
    grid = Mesh(mesh.devices.reshape(mesh.shape["tm"], 4, 4, 2), ("tm", "z", "x", "c"))
    tp = ("z", "x", "c")
    return jax.shard_map(
        on_device,
        mesh=grid,
        in_specs=(P("tm", None, None, tp), P(None, None, None, None, tp), P(), P()),
        out_specs=P("tm", tp, None, None),
        check_vma=False,
    )
```

```python
import functools

import jax
import jax.numpy as jnp
from jax import lax
from jax.experimental import pallas as pl
from jax.experimental.pallas import tpu as pltpu
from jax.sharding import Mesh, PartitionSpec as P

PITCH = 32
LANES = 128
QUARTERS = 4
BF16 = jnp.bfloat16
F32 = jnp.float32
SMEM = pl.BlockSpec(memory_space=pltpu.SMEM)
HBM = pl.BlockSpec(memory_space=pltpu.HBM)
VMEM = pl.BlockSpec(memory_space=pltpu.VMEM)
LIMIT = 20 * 2**20


def call(kernel, out_shape, operands, scratch=(), specs=None):
    specs = specs or [SMEM] + [VMEM] * (len(operands) - 1)
    return pl.pallas_call(
        kernel,
        out_shape=out_shape,
        in_specs=specs,
        out_specs=jax.tree.map(lambda _: VMEM, out_shape),
        scratch_shapes=scratch,
        compiler_params=pltpu.CompilerParams(vmem_limit_bytes=LIMIT),
    )(*operands)


def silu(v):
    return v / (1.0 + jnp.exp(-v))


def column_mask(shape, axis, across):
    return lax.rem(lax.broadcasted_iota(jnp.int32, shape, axis), PITCH) < across


def before(block):
    lane = lax.broadcasted_iota(jnp.int32, block.shape, 1)
    return jnp.where(lane >= PITCH, pltpu.roll(block, PITCH, 1), 0.0)


def after(block):
    lane = lax.broadcasted_iota(jnp.int32, block.shape, 1)
    return jnp.where(lane < LANES - PITCH, pltpu.roll(block, LANES - PITCH, 1), 0.0)


def pack_kernel(field_ref, weight_ref, packed_ref, act_ref, slices_ref, raw_ref, columns_ref, rows_ref, sems):
    across, shard, height = field_ref.shape
    deep = height // QUARTERS
    load = pltpu.make_async_copy(field_ref, raw_ref, sems.at[4])
    load.start()
    width = weight_ref.shape[1] // 4
    copies = []
    for d in range(4):
        source = weight_ref.at[:, d * width : (d + 1) * width]
        copies.append(pltpu.make_async_copy(source, slices_ref.at[d], sems.at[d]))
        copies[d].start()
    columns_ref[...] = jnp.zeros(columns_ref.shape, F32)
    load.wait()
    columns_ref[: across * shard, :height] = raw_ref[...].astype(F32).reshape(across * shard, height)
    for c in range(shard):
        cells = columns_ref[pl.ds(c, PITCH, stride=shard), :].T
        quarters = [cells[q * deep : (q + 1) * deep] for q in range(QUARTERS)]
        rows_ref[pl.ds(c, deep, stride=shard), :] = jnp.concatenate(quarters, 1)
    for v in range(deep):
        values = rows_ref[v * shard : (v + 1) * shard, :]
        packed_ref[:, v * LANES : (v + 1) * LANES] = values.astype(BF16)
        act_ref[:, v * LANES : (v + 1) * LANES] = silu(values).astype(BF16)
    for copy in copies:
        copy.wait()


def coarse_kernel(at_ref, field_ref, slices_ref, *refs):
    blocks, (out_ref, all_ref, taps_ref, sum_ref) = refs[:8], refs[8:]
    shard, cells = field_ref.shape
    deep = cells // LANES
    group = 8 * shard
    wide = 4 * shard
    z, x, c, t = at_ref[0], at_ref[1], at_ref[2], at_ref[3]
    for n, block in enumerate(blocks):
        x_from = lax.rem(x + 4 - n // 2, 4)
        c_from = c if n % 2 == 0 else 1 - c
        base = (x_from * 2 + c_from) * shard
        for k in range(3):
            part = pl.multiple_of(jnp.minimum(t, 2 - k) * shard, shard)
            all_ref[pl.ds(pl.multiple_of(k * group + base, shard), shard), LANES : LANES + cells] = block[
                pl.ds(part, shard), :
            ]
    first, last = all_ref[:, LANES : 2 * LANES], all_ref[:, cells : cells + LANES]
    all_ref[:, :LANES] = before(last.astype(F32)).astype(BF16)
    all_ref[:, LANES + cells :] = after(first.astype(F32)).astype(BF16)
    for d in range(4):
        for k in range(3):
            for i in range(3):
                for j in range(3):
                    tap = (k * 3 + i) * 3 + j
                    to = j * wide + d * shard
                    taps_ref[i, to : to + shard, k * group : (k + 1) * group] = slices_ref[
                        d, tap * shard : (tap + 1) * shard, :
                    ]
    span = 4 * LANES
    for n in range(cells // span):
        total = None
        for i in range(3):
            lo = i * LANES + n * span
            part = jnp.dot(taps_ref[i], all_ref[:, lo : lo + span], preferred_element_type=F32)
            total = part if total is None else total + part
        for v in range(4):
            left, here, right = (total[j * wide : (j + 1) * wide, v * LANES : (v + 1) * LANES] for j in range(3))
            lo = LANES + n * span + v * LANES
            sum_ref[:, lo : lo + LANES] = pltpu.roll(left, 1, 1) + here + pltpu.roll(right, LANES - 1, 1)
    own = pl.ds(pl.multiple_of(z * shard, shard), shard)
    sum_ref[own, LANES : LANES + cells] = sum_ref[own, LANES : LANES + cells] + field_ref[...].astype(F32)
    sum_ref[:, :LANES] = before(sum_ref[:, cells : cells + LANES])
    sum_ref[:, LANES + cells :] = after(sum_ref[:, LANES : 2 * LANES])
    at = lax.broadcasted_iota(jnp.int32, (wide, LANES), 1) // PITCH
    for m in range(deep // 2):
        rows = [sum_ref[:, (2 * m + r) * LANES : (2 * m + r + 1) * LANES] for r in range(4)]
        for q in range(QUARTERS):
            moved = [pltpu.roll(rows[r], (r - q) % 4 * PITCH, 1) if r != q else rows[r] for r in range(4)]
            strip = jnp.where(at < 2, jnp.where(at < 1, moved[0], moved[1]), jnp.where(at < 3, moved[2], moved[3]))
            out_ref[q * (deep // 2) + m] = strip.astype(BF16)


def strip_kernel(across, parts_ref, out_ref, order_ref):
    shard = parts_ref.shape[1] // 4
    for n in range(8):
        total = None
        for z in range(4):
            part = parts_ref[z * 8 + n].astype(F32)
            total = part if total is None else total + part
        act = silu(total.astype(BF16).astype(F32))
        act = jnp.where(column_mask(act.shape, 1, across), act, 0.0)
        for z in range(4):
            order_ref[(z * 8 + n) * shard : (z * 8 + n + 1) * shard, :] = act[z * shard : (z + 1) * shard]
    out_ref[...] = order_ref[...].T.astype(BF16)


def down(v):
    return pltpu.roll(v, 1, 0)


def up(v):
    return pltpu.roll(v, v.shape[0] - 1, 0)


def fine_kernel(across, at_ref, a0_ref, a1_ref, a2_ref, wide_ref, last_ref, first_ref, second_ref, own_ref):
    t, strip, strips = at_ref[3], at_ref[4], at_ref[5]
    a0 = a0_ref[...].astype(F32)
    a1 = jnp.where(t >= 1, a1_ref[...].astype(F32), a0)
    a2 = jnp.where(t >= 2, a2_ref[...].astype(F32), a1)
    frames = jnp.concatenate([a2, a1, a0], 1).astype(BF16)
    spans = ((0, 3), (0, 4), (1, 4))
    maps = ((0, 0, 1, 1, 2, 2), (0, 1, 1, 2, 2, 3), (0, 0, 1, 1, 2, 2))
    even, odd = [None] * 6, [None] * 6
    for i in range(3):
        lo, hi = spans[i]
        sums = []
        for j in range(3):
            sums.append(
                jnp.dot(frames[lo * PITCH : hi * PITCH], wide_ref[i * 3 + j], preferred_element_type=F32)
            )
        at_even = down(sums[0]) + sums[1] + sums[2]
        at_odd = sums[0] + sums[1] + up(sums[2])
        for r in range(6):
            at = slice(maps[i][r] * PITCH, (maps[i][r] + 1) * PITCH)
            even[r] = at_even[at] if even[r] is None else even[r] + at_even[at]
            odd[r] = at_odd[at] if odd[r] is None else odd[r] + at_odd[at]
    mid = [jnp.concatenate(rows, 0).astype(BF16).astype(F32) for rows in (even, odd)]
    shape = mid[0].shape
    row = lax.broadcasted_iota(jnp.int32, shape, 0) // PITCH
    keep = column_mask(shape, 0, across)
    keep = keep & ((row > 0) | (strip > 0)) & ((row < 5) | (strip < strips - 1))
    acts = [jnp.where(keep, silu(m), 0.0).astype(BF16) for m in mid]
    size = 4 * PITCH
    sums = []
    for k in range(3):
        parts = []
        for j in range(3):
            total = None
            for i in range(3):
                rows = slice(i * PITCH, i * PITCH + size)
                both = jnp.concatenate([acts[0][rows], acts[1][rows]], 0)
                part = jnp.dot(both, last_ref[k, i, j], preferred_element_type=F32)
                total = part if total is None else total + part
            parts.append(total)
        at_even = down(parts[0][size:]) + parts[1][:size] + parts[2][size:]
        at_odd = parts[0][:size] + parts[1][size:] + up(parts[2][:size])
        sums.append(jnp.concatenate([at_even, at_odd], 0))
    start = t == 0
    late = sums[0] + sums[1]
    first_ref[...] = jnp.where(start, late, sums[1]).astype(BF16)
    second_ref[...] = sums[0].astype(BF16)
    rows = slice(PITCH, PITCH + size)
    own = jnp.concatenate([mid[0][rows], mid[1][rows]], 0) + sums[2]
    own_ref[...] = jnp.where(start, own + late, own)


def last_kernel(across, at_ref, own_ref, first_ref, second_ref, out_ref, order_ref):
    t = at_ref[3]
    zero = jnp.zeros(own_ref.shape, F32)
    total = (
        own_ref[...]
        + jnp.where(t >= 1, first_ref[...].astype(F32), zero)
        + jnp.where(t >= 2, second_ref[...].astype(F32), zero)
    )
    for parity in range(2):
        for h in range(4):
            at = (parity * 4 + h) * PITCH
            for half in range(2):
                order_ref[half, pl.ds(4 * parity + h, PITCH, stride=8), :] = total[
                    at : at + PITCH, 128 * half : 128 * half + 128
                ]
    for half in range(2):
        out_ref[:, 128 * half : 128 * half + 128] = order_ref[half, : 4 * across * 2].astype(BF16)


def turned(block, axis, distance):
    count = lax.axis_size(axis)
    return lax.ppermute(block, axis, [(i, (i + distance) % count) for i in range(count)])


def on_device(features, weight_one, weight_two, weight_three):
    own_block = features[0]
    height, across, shard = own_block.shape
    channels = weight_one.shape[3]
    cells = height * PITCH
    tp = ("z", "x", "c")
    at = jnp.stack(
        [lax.axis_index(a) for a in ("z", "x", "c", "tm")] + [lax.axis_index(tp), lax.axis_size(tp)]
    ).astype(jnp.int32)
    kernel = jnp.transpose(weight_one, (0, 1, 2, 4, 3)).reshape(27 * shard, channels)
    small = jax.ShapeDtypeStruct((shard, cells), BF16)
    field, act_in, slices = call(
        pack_kernel,
        (small, small, jax.ShapeDtypeStruct((4, 27 * shard, channels // 4), BF16)),
        tuple(pltpu.with_memory_space_constraint(a, pltpu.HBM) for a in (jnp.transpose(own_block, (1, 2, 0)), kernel)),
        (
            pltpu.VMEM((across, shard, height), BF16),
            pltpu.VMEM((PITCH * shard, LANES), F32),
            pltpu.VMEM((cells // LANES * shard, LANES), F32),
            pltpu.SemaphoreType.DMA((5,)),
        ),
        [HBM, HBM],
    )
    frames = jnp.concatenate([act_in, turned(act_in, "tm", 1), turned(act_in, "tm", 2)], 0)
    slices = lax.all_to_all(slices, "z", 0, 0, tiled=True)
    blocks = []
    for d in range(4):
        block = turned(frames, "x", d) if d else frames
        blocks += [block, turned(block, "c", 1)]
    strips = lax.axis_size(tp)
    cut = call(
        coarse_kernel,
        jax.ShapeDtypeStruct((strips, 4 * shard, LANES), BF16),
        (at, field, slices, *blocks),
        (
            pltpu.VMEM((3 * channels // 4, cells + 2 * LANES), BF16),
            pltpu.VMEM((3, 12 * shard, 3 * channels // 4), BF16),
            pltpu.VMEM((4 * shard, cells + 2 * LANES), F32),
        ),
    )
    parts = lax.all_to_all(cut, tp, 0, 0, tiled=True)
    strip = pl.pallas_call(
        functools.partial(strip_kernel, across),
        out_shape=jax.ShapeDtypeStruct((LANES, channels), BF16),
        scratch_shapes=[pltpu.VMEM((channels, LANES), F32)],
        compiler_params=pltpu.CompilerParams(vmem_limit_bytes=LIMIT),
    )(parts)
    width = weight_two.shape[4]
    wide = jnp.transpose(weight_two, (1, 2, 0, 3, 4)).reshape(9, 3 * channels, width)
    small = jax.ShapeDtypeStruct((8 * PITCH, width), BF16)
    first, second, own = call(
        functools.partial(fine_kernel, across),
        (small, small, jax.ShapeDtypeStruct((8 * PITCH, width), F32)),
        (at, strip, turned(strip, "tm", 1), turned(strip, "tm", 2), wide, weight_three),
    )
    decoded = call(
        functools.partial(last_kernel, across),
        jax.ShapeDtypeStruct((8 * across, width), BF16),
        (at, own, turned(first, "tm", 1), turned(second, "tm", 2)),
        (pltpu.VMEM((2, 8 * PITCH, 128), F32),),
    )
    return jnp.transpose(decoded.reshape(2 * across, 4, width), (1, 0, 2))[None]


def solution(mesh):
    grid = Mesh(mesh.devices.reshape(mesh.shape["tm"], 4, 4, 2), ("tm", "z", "x", "c"))
    tp = ("z", "x", "c")
    return jax.shard_map(
        on_device,
        mesh=grid,
        in_specs=(P("tm", None, None, tp), P(None, None, None, None, tp), P(), P()),
        out_specs=P("tm", tp, None, None),
        check_vma=False,
    )
```

```python
import functools

import jax
import jax.numpy as jnp
from jax import lax
from jax.experimental import pallas as pl
from jax.experimental.pallas import tpu as pltpu
from jax.sharding import Mesh, PartitionSpec as P

PITCH = 32
LANES = 128
QUARTERS = 4
BF16 = jnp.bfloat16
F32 = jnp.float32
SMEM = pl.BlockSpec(memory_space=pltpu.SMEM)
HBM = pl.BlockSpec(memory_space=pltpu.HBM)
VMEM = pl.BlockSpec(memory_space=pltpu.VMEM)
LIMIT = 20 * 2**20


def call(kernel, out_shape, operands, scratch=(), specs=None):
    specs = specs or [SMEM] + [VMEM] * (len(operands) - 1)
    return pl.pallas_call(
        kernel,
        out_shape=out_shape,
        in_specs=specs,
        out_specs=jax.tree.map(lambda _: VMEM, out_shape),
        scratch_shapes=scratch,
        compiler_params=pltpu.CompilerParams(vmem_limit_bytes=LIMIT),
    )(*operands)


def silu(v):
    return v / (1.0 + jnp.exp(-v))


def column_mask(shape, axis, across):
    return lax.rem(lax.broadcasted_iota(jnp.int32, shape, axis), PITCH) < across


def before(block):
    lane = lax.broadcasted_iota(jnp.int32, block.shape, 1)
    return jnp.where(lane >= PITCH, pltpu.roll(block, PITCH, 1), 0.0)


def after(block):
    lane = lax.broadcasted_iota(jnp.int32, block.shape, 1)
    return jnp.where(lane < LANES - PITCH, pltpu.roll(block, LANES - PITCH, 1), 0.0)


def pack_kernel(field_ref, weight_ref, packed_ref, act_ref, slices_ref, raw_ref, columns_ref, rows_ref, sems):
    across, shard, height = field_ref.shape
    deep = height // QUARTERS
    load = pltpu.make_async_copy(field_ref, raw_ref, sems.at[4])
    load.start()
    width = weight_ref.shape[1] // 4
    copies = []
    for d in range(4):
        source = weight_ref.at[:, d * width : (d + 1) * width]
        copies.append(pltpu.make_async_copy(source, slices_ref.at[d], sems.at[d]))
        copies[d].start()
    columns_ref[...] = jnp.zeros(columns_ref.shape, F32)
    load.wait()
    columns_ref[: across * shard, :height] = raw_ref[...].astype(F32).reshape(across * shard, height)
    for c in range(shard):
        cells = columns_ref[pl.ds(c, PITCH, stride=shard), :].T
        quarters = [cells[q * deep : (q + 1) * deep] for q in range(QUARTERS)]
        rows_ref[pl.ds(c, deep, stride=shard), :] = jnp.concatenate(quarters, 1)
    for v in range(deep):
        values = rows_ref[v * shard : (v + 1) * shard, :]
        packed_ref[:, v * LANES : (v + 1) * LANES] = values.astype(BF16)
        act_ref[:, v * LANES : (v + 1) * LANES] = silu(values).astype(BF16)
    for copy in copies:
        copy.wait()


def coarse_kernel(at_ref, field_ref, slices_ref, *refs):
    blocks, (out_ref, all_ref, taps_ref, sum_ref) = refs[:8], refs[8:]
    shard, cells = field_ref.shape
    deep = cells // LANES
    group = 8 * shard
    wide = 4 * shard
    z, x, c, t = at_ref[0], at_ref[1], at_ref[2], at_ref[3]
    for n, block in enumerate(blocks):
        x_from = lax.rem(x + 4 - n // 2, 4)
        c_from = c if n % 2 == 0 else 1 - c
        base = (x_from * 2 + c_from) * shard
        for k in range(3):
            part = pl.multiple_of(jnp.minimum(t, 2 - k) * shard, shard)
            all_ref[pl.ds(pl.multiple_of(k * group + base, shard), shard), LANES : LANES + cells] = block[
                pl.ds(part, shard), :
            ]
    first, last = all_ref[:, LANES : 2 * LANES], all_ref[:, cells : cells + LANES]
    all_ref[:, :LANES] = before(last.astype(F32)).astype(BF16)
    all_ref[:, LANES + cells :] = after(first.astype(F32)).astype(BF16)
    for d in range(4):
        for k in range(3):
            for i in range(3):
                for j in range(3):
                    tap = (k * 3 + i) * 3 + j
                    to = j * wide + d * shard
                    taps_ref[i, to : to + shard, k * group : (k + 1) * group] = slices_ref[
                        d, tap * shard : (tap + 1) * shard, :
                    ]
    span = 4 * LANES
    for n in range(cells // span):
        total = None
        for i in range(3):
            lo = i * LANES + n * span
            part = jnp.dot(taps_ref[i], all_ref[:, lo : lo + span], preferred_element_type=F32)
            total = part if total is None else total + part
        for v in range(4):
            left, here, right = (total[j * wide : (j + 1) * wide, v * LANES : (v + 1) * LANES] for j in range(3))
            lo = LANES + n * span + v * LANES
            sum_ref[:, lo : lo + LANES] = pltpu.roll(left, 1, 1) + here + pltpu.roll(right, LANES - 1, 1)
    own = pl.ds(pl.multiple_of(z * shard, shard), shard)
    sum_ref[own, LANES : LANES + cells] = sum_ref[own, LANES : LANES + cells] + field_ref[...].astype(F32)
    sum_ref[:, :LANES] = before(sum_ref[:, cells : cells + LANES])
    sum_ref[:, LANES + cells :] = after(sum_ref[:, LANES : 2 * LANES])
    at = lax.broadcasted_iota(jnp.int32, (wide, LANES), 1) // PITCH
    half = wide // 2

    def placed(pieces, q):
        moved = [pltpu.roll(p, (r - q) % 4 * PITCH, 1) if r != q else p for r, p in enumerate(pieces)]
        to = at[: pieces[0].shape[0]]
        return jnp.where(to < 2, jnp.where(to < 1, moved[0], moved[1]), jnp.where(to < 3, moved[2], moved[3]))

    for m in range(deep // 4):
        rows = [sum_ref[:, (4 * m + r) * LANES : (4 * m + r + 1) * LANES] for r in range(6)]
        rest = [rows[4][:half], rows[5][:half], rows[4][half:], rows[5][half:]]
        for q in range(QUARTERS):
            out_ref[q * (deep // 4) + m, :wide] = placed(rows[:4], q).astype(BF16)
            out_ref[q * (deep // 4) + m, wide:] = placed(rest, q).astype(BF16)


def strip_kernel(across, parts_ref, out_ref, order_ref):
    wide = parts_ref.shape[1] * 2 // 3
    shard = wide // 4
    order_ref[:, LANES:] = jnp.zeros((order_ref.shape[0], LANES), F32)
    for n in range(4):
        total = None
        for z in range(4):
            part = parts_ref[z * 4 + n].astype(F32)
            total = part if total is None else total + part
        act = silu(total.astype(BF16).astype(F32))
        act = jnp.where(column_mask(act.shape, 1, across), act, 0.0)
        rest = [act[wide:], pltpu.roll(act[wide:], LANES // 2, 1)]
        for z in range(4):
            to = slice((z * 4 + n) * shard, (z * 4 + n + 1) * shard)
            order_ref[to, :LANES] = act[z * shard : (z + 1) * shard]
            order_ref[to, LANES : LANES + LANES // 2] = rest[z // 2][z % 2 * shard : (z % 2 + 1) * shard, : LANES // 2]
    out_ref[...] = order_ref[...].T[: out_ref.shape[0]].astype(BF16)


def stage_kernel(weight_ref, tie_ref, out_ref, sems):
    copies = []
    for n in range(18):
        i, j, c = n // 6, n // 2 % 3, n % 2
        copies.append(pltpu.make_async_copy(weight_ref.at[:, i, j, :, c], out_ref.at[n // 2, :, c], sems.at[n]))
    for copy in copies:
        copy.start()
    for copy in copies:
        copy.wait()


def down(v):
    return pltpu.roll(v, 1, 0)


def up(v):
    return pltpu.roll(v, v.shape[0] - 1, 0)


def fine_kernel(across, at_ref, *refs):
    halves, (wide_ref, last_ref, first_ref, second_ref, own_ref, frames_ref) = refs[:6], refs[6:]
    c, t, strip, strips = at_ref[2], at_ref[3], at_ref[4], at_ref[5]
    cells, channels, width = 4 * PITCH, halves[0].shape[1] * 2, own_ref.shape[1]
    rows = pl.ds(pl.multiple_of(c * 2 * PITCH, 2 * PITCH), cells)

    def put(k, part):
        for n, side in enumerate((c, 1 - c)):
            to = pl.multiple_of(k * channels + side * (channels // 2), channels // 2)
            frames_ref[:, pl.ds(to, channels // 2)] = halves[2 * part + n][rows, :]

    put(2, 0)
    for k in range(2):
        for part in range(3 - k):
            pl.when(jnp.minimum(t, 2 - k) == part)(functools.partial(put, k, part))
    frames = frames_ref[...]
    spans = ((0, 3), (0, 4), (1, 4))
    maps = ((0, 0, 1, 1, 2, 2), (0, 1, 1, 2, 2, 3), (0, 0, 1, 1, 2, 2))
    even, odd = [None] * 6, [None] * 6
    for i in range(3):
        lo, hi = spans[i]
        sums = []
        for j in range(3):
            sums.append(
                jnp.dot(frames[lo * PITCH : hi * PITCH], wide_ref[i * 3 + j].reshape(3 * channels, width), preferred_element_type=F32)
            )
        at_even = down(sums[0]) + sums[1] + sums[2]
        at_odd = sums[0] + sums[1] + up(sums[2])
        for r in range(6):
            at = slice(maps[i][r] * PITCH, (maps[i][r] + 1) * PITCH)
            even[r] = at_even[at] if even[r] is None else even[r] + at_even[at]
            odd[r] = at_odd[at] if odd[r] is None else odd[r] + at_odd[at]
    mid = [jnp.concatenate(rows, 0).astype(BF16).astype(F32) for rows in (even, odd)]
    shape = mid[0].shape
    row = lax.broadcasted_iota(jnp.int32, shape, 0) // PITCH
    keep = column_mask(shape, 0, across)
    keep = keep & ((row > 0) | (strip > 0)) & ((row < 5) | (strip < strips - 1))
    acts = [jnp.where(keep, silu(m), 0.0).astype(BF16) for m in mid]
    size = 4 * PITCH
    sums = []
    for k in range(3):
        parts = []
        for j in range(3):
            total = None
            for i in range(3):
                rows = slice(i * PITCH, i * PITCH + size)
                both = jnp.concatenate([acts[0][rows], acts[1][rows]], 0)
                part = jnp.dot(both, last_ref[k, i, j], preferred_element_type=F32)
                total = part if total is None else total + part
            parts.append(total)
        at_even = down(parts[0][size:]) + parts[1][:size] + parts[2][size:]
        at_odd = parts[0][:size] + parts[1][size:] + up(parts[2][:size])
        sums.append(jnp.concatenate([at_even, at_odd], 0))
    start = t == 0
    late = sums[0] + sums[1]
    first_ref[...] = jnp.where(start, late, sums[1]).astype(BF16)
    second_ref[...] = sums[0].astype(BF16)
    rows = slice(PITCH, PITCH + size)
    own = jnp.concatenate([mid[0][rows], mid[1][rows]], 0) + sums[2]
    own_ref[...] = jnp.where(start, own + late, own)


def last_kernel(across, at_ref, own_ref, first_ref, second_ref, out_ref, order_ref):
    t = at_ref[3]
    zero = jnp.zeros(own_ref.shape, F32)
    total = (
        own_ref[...]
        + jnp.where(t >= 1, first_ref[...].astype(F32), zero)
        + jnp.where(t >= 2, second_ref[...].astype(F32), zero)
    )
    for parity in range(2):
        for h in range(4):
            at = (parity * 4 + h) * PITCH
            for half in range(2):
                order_ref[half, pl.ds(4 * parity + h, PITCH, stride=8), :] = total[
                    at : at + PITCH, 128 * half : 128 * half + 128
                ]
    for half in range(2):
        out_ref[:, 128 * half : 128 * half + 128] = order_ref[half, : 4 * across * 2].astype(BF16)


def turned(block, axis, distance):
    count = lax.axis_size(axis)
    return lax.ppermute(block, axis, [(i, (i + distance) % count) for i in range(count)])


def on_device(features, weight_one, weight_two, weight_three):
    own_block = features[0]
    height, across, shard = own_block.shape
    channels = weight_one.shape[3]
    cells = height * PITCH
    tp = ("z", "x", "c")
    at = jnp.stack(
        [lax.axis_index(a) for a in ("z", "x", "c", "tm")] + [lax.axis_index(tp), lax.axis_size(tp)]
    ).astype(jnp.int32)
    kernel = jnp.transpose(weight_one, (0, 1, 2, 4, 3)).reshape(27 * shard, channels)
    small = jax.ShapeDtypeStruct((shard, cells), BF16)
    field, act_in, slices = call(
        pack_kernel,
        (small, small, jax.ShapeDtypeStruct((4, 27 * shard, channels // 4), BF16)),
        tuple(pltpu.with_memory_space_constraint(a, pltpu.HBM) for a in (jnp.transpose(own_block, (1, 2, 0)), kernel)),
        (
            pltpu.VMEM((across, shard, height), BF16),
            pltpu.VMEM((PITCH * shard, LANES), F32),
            pltpu.VMEM((cells // LANES * shard, LANES), F32),
            pltpu.SemaphoreType.DMA((5,)),
        ),
        [HBM, HBM],
    )
    frames = jnp.concatenate([act_in, turned(act_in, "tm", 1), turned(act_in, "tm", 2)], 0)
    slices = lax.all_to_all(slices, "z", 0, 0, tiled=True)
    blocks = []
    for d in range(4):
        block = turned(frames, "x", d) if d else frames
        blocks += [block, turned(block, "c", 1)]
    cut = call(
        coarse_kernel,
        jax.ShapeDtypeStruct((16, 6 * shard, LANES), BF16),
        (at, field, slices, *blocks),
        (
            pltpu.VMEM((3 * channels // 4, cells + 2 * LANES), BF16),
            pltpu.VMEM((3, 12 * shard, 3 * channels // 4), BF16),
            pltpu.VMEM((4 * shard, cells + 2 * LANES), F32),
        ),
    )
    parts = lax.all_to_all(cut, ("z", "x"), 0, 0, tiled=True)
    own = pl.pallas_call(
        functools.partial(strip_kernel, across),
        out_shape=jax.ShapeDtypeStruct((6 * PITCH, channels // 2), BF16),
        scratch_shapes=[pltpu.VMEM((channels // 2, 2 * LANES), F32)],
        compiler_params=pltpu.CompilerParams(vmem_limit_bytes=LIMIT),
    )(parts)
    width = weight_two.shape[4]
    wide = call(
        stage_kernel,
        jax.ShapeDtypeStruct((9, 3, 2, channels // 2 // shard, shard, width), BF16),
        (pltpu.with_memory_space_constraint(weight_two.reshape(3, 3, 3, -1, 2, shard, width), pltpu.HBM), own),
        (pltpu.SemaphoreType.DMA((18,)),),
        [HBM, pl.BlockSpec(memory_space=pl.ANY)],
    )
    moved = [turned(own, "tm", d) for d in (1, 2)]
    wide, *moved = lax.optimization_barrier((wide, *moved))
    halves = []
    for half in (own, *moved):
        halves += [half, turned(half, "c", 1)]
    small = jax.ShapeDtypeStruct((8 * PITCH, width), BF16)
    first, second, own = call(
        functools.partial(fine_kernel, across),
        (small, small, jax.ShapeDtypeStruct((8 * PITCH, width), F32)),
        (at, *halves, wide, weight_three),
        (pltpu.VMEM((4 * PITCH, 3 * channels), BF16),),
    )
    decoded = call(
        functools.partial(last_kernel, across),
        jax.ShapeDtypeStruct((8 * across, width), BF16),
        (at, own, turned(first, "tm", 1), turned(second, "tm", 2)),
        (pltpu.VMEM((2, 8 * PITCH, 128), F32),),
    )
    return jnp.transpose(decoded.reshape(2 * across, 4, width), (1, 0, 2))[None]


def solution(mesh):
    grid = Mesh(mesh.devices.reshape(mesh.shape["tm"], 4, 4, 2), ("tm", "z", "x", "c"))
    tp = ("z", "x", "c")
    return jax.shard_map(
        on_device,
        mesh=grid,
        in_specs=(P("tm", None, None, tp), P(None, None, None, None, tp), P(), P()),
        out_specs=P("tm", tp, None, None),
        check_vma=False,
    )
```

```python
import functools

import jax
import jax.numpy as jnp
from jax import lax
from jax.experimental import pallas as pl
from jax.experimental.pallas import tpu as pltpu
from jax.sharding import Mesh, PartitionSpec as P

PITCH = 32
LANES = 128
QUARTERS = 4
BF16 = jnp.bfloat16
F32 = jnp.float32
SMEM = pl.BlockSpec(memory_space=pltpu.SMEM)
HBM = pl.BlockSpec(memory_space=pltpu.HBM)
VMEM = pl.BlockSpec(memory_space=pltpu.VMEM)
LIMIT = 20 * 2**20


def call(kernel, out_shape, operands, scratch=(), specs=None):
    specs = specs or [SMEM] + [VMEM] * (len(operands) - 1)
    return pl.pallas_call(
        kernel,
        out_shape=out_shape,
        in_specs=specs,
        out_specs=jax.tree.map(lambda _: VMEM, out_shape),
        scratch_shapes=scratch,
        compiler_params=pltpu.CompilerParams(vmem_limit_bytes=LIMIT),
    )(*operands)


def silu(v):
    return v / (1.0 + jnp.exp(-v))


def column_mask(shape, axis, across):
    return lax.rem(lax.broadcasted_iota(jnp.int32, shape, axis), PITCH) < across


def before(block):
    lane = lax.broadcasted_iota(jnp.int32, block.shape, 1)
    return jnp.where(lane >= PITCH, pltpu.roll(block, PITCH, 1), 0.0)


def after(block):
    lane = lax.broadcasted_iota(jnp.int32, block.shape, 1)
    return jnp.where(lane < LANES - PITCH, pltpu.roll(block, LANES - PITCH, 1), 0.0)


def pack_kernel(field_ref, weight_ref, packed_ref, act_ref, slices_ref, raw_ref, columns_ref, rows_ref, sems):
    across, shard, height = field_ref.shape
    deep = height // QUARTERS
    load = pltpu.make_async_copy(field_ref, raw_ref, sems.at[4])
    load.start()
    width = weight_ref.shape[1] // 4
    copies = []
    for d in range(4):
        source = weight_ref.at[:, d * width : (d + 1) * width]
        copies.append(pltpu.make_async_copy(source, slices_ref.at[d], sems.at[d]))
        copies[d].start()
    columns_ref[...] = jnp.zeros(columns_ref.shape, F32)
    load.wait()
    columns_ref[: across * shard, :height] = raw_ref[...].astype(F32).reshape(across * shard, height)
    for c in range(shard):
        cells = columns_ref[pl.ds(c, PITCH, stride=shard), :].T
        quarters = [cells[q * deep : (q + 1) * deep] for q in range(QUARTERS)]
        rows_ref[pl.ds(c, deep, stride=shard), :] = jnp.concatenate(quarters, 1)
    for v in range(deep):
        values = rows_ref[v * shard : (v + 1) * shard, :]
        packed_ref[:, v * LANES : (v + 1) * LANES] = values.astype(BF16)
        act_ref[:, v * LANES : (v + 1) * LANES] = silu(values).astype(BF16)
    for copy in copies:
        copy.wait()


def coarse_kernel(at_ref, field_ref, slices_ref, *refs):
    blocks, (out_ref, all_ref, taps_ref, sum_ref) = refs[:8], refs[8:]
    shard, cells = field_ref.shape
    deep = cells // LANES
    group = 8 * shard
    wide = 4 * shard
    z, x, c, t = at_ref[0], at_ref[1], at_ref[2], at_ref[3]
    for n, block in enumerate(blocks):
        x_from = lax.rem(x + 4 - n // 2, 4)
        c_from = c if n % 2 == 0 else 1 - c
        base = (x_from * 2 + c_from) * shard
        for k in range(3):
            part = pl.multiple_of(jnp.minimum(t, 2 - k) * shard, shard)
            all_ref[pl.ds(pl.multiple_of(k * group + base, shard), shard), LANES : LANES + cells] = block[
                pl.ds(part, shard), :
            ]
    first, last = all_ref[:, LANES : 2 * LANES], all_ref[:, cells : cells + LANES]
    all_ref[:, :LANES] = before(last.astype(F32)).astype(BF16)
    all_ref[:, LANES + cells :] = after(first.astype(F32)).astype(BF16)
    for d in range(4):
        for k in range(3):
            for i in range(3):
                for j in range(3):
                    tap = (k * 3 + i) * 3 + j
                    to = j * wide + d * shard
                    taps_ref[i, to : to + shard, k * group : (k + 1) * group] = slices_ref[
                        d, tap * shard : (tap + 1) * shard, :
                    ]
    span = 4 * LANES
    for n in range(cells // span):
        total = None
        for i in range(3):
            lo = i * LANES + n * span
            part = jnp.dot(taps_ref[i], all_ref[:, lo : lo + span], preferred_element_type=F32)
            total = part if total is None else total + part
        for v in range(4):
            left, here, right = (total[j * wide : (j + 1) * wide, v * LANES : (v + 1) * LANES] for j in range(3))
            lo = LANES + n * span + v * LANES
            sum_ref[:, lo : lo + LANES] = pltpu.roll(left, 1, 1) + here + pltpu.roll(right, LANES - 1, 1)
    own = pl.ds(pl.multiple_of(z * shard, shard), shard)
    sum_ref[own, LANES : LANES + cells] = sum_ref[own, LANES : LANES + cells] + field_ref[...].astype(F32)
    sum_ref[:, :LANES] = before(sum_ref[:, cells : cells + LANES])
    sum_ref[:, LANES + cells :] = after(sum_ref[:, LANES : 2 * LANES])
    at = lax.broadcasted_iota(jnp.int32, (wide, LANES), 1) // PITCH
    half = wide // 2

    def placed(pieces, q):
        moved = [pltpu.roll(p, (r - q) % 4 * PITCH, 1) if r != q else p for r, p in enumerate(pieces)]
        to = at[: pieces[0].shape[0]]
        return jnp.where(to < 2, jnp.where(to < 1, moved[0], moved[1]), jnp.where(to < 3, moved[2], moved[3]))

    for m in range(deep // 4):
        rows = [sum_ref[:, (4 * m + r) * LANES : (4 * m + r + 1) * LANES] for r in range(6)]
        rest = [rows[4][:half], rows[5][:half], rows[4][half:], rows[5][half:]]
        for q in range(QUARTERS):
            out_ref[q * (deep // 4) + m, :wide] = placed(rows[:4], q).astype(BF16)
            out_ref[q * (deep // 4) + m, wide:] = placed(rest, q).astype(BF16)


def strip_kernel(across, parts_ref, out_ref, order_ref):
    wide = parts_ref.shape[1] * 2 // 3
    shard = wide // 4
    order_ref[:, LANES:] = jnp.zeros((order_ref.shape[0], LANES), F32)
    for n in range(4):
        total = None
        for z in range(4):
            part = parts_ref[z * 4 + n].astype(F32)
            total = part if total is None else total + part
        act = silu(total.astype(BF16).astype(F32))
        act = jnp.where(column_mask(act.shape, 1, across), act, 0.0)
        rest = [act[wide:], pltpu.roll(act[wide:], LANES // 2, 1)]
        for z in range(4):
            to = slice((z * 4 + n) * shard, (z * 4 + n + 1) * shard)
            order_ref[to, :LANES] = act[z * shard : (z + 1) * shard]
            order_ref[to, LANES : LANES + LANES // 2] = rest[z // 2][z % 2 * shard : (z % 2 + 1) * shard, : LANES // 2]
    out_ref[...] = order_ref[...].T[: out_ref.shape[0]].astype(BF16)


def stage_kernel(at_ref, weight_ref, tie_ref, out_ref, sems):
    c = at_ref[2]
    copies = []
    for n in range(9):
        copies.append(pltpu.make_async_copy(weight_ref.at[:, n // 3, n % 3, :, c], out_ref.at[n], sems.at[n]))
        copies[n].start()
    for copy in copies:
        copy.wait()


def down(v):
    return pltpu.roll(v, 1, 0)


def up(v):
    return pltpu.roll(v, v.shape[0] - 1, 0)


def wide_kernel(at_ref, own_ref, first_ref, second_ref, wide_ref, keep_ref, send_ref, frames_ref, sum_ref):
    c, t = at_ref[2], at_ref[3]
    halves = (own_ref, first_ref, second_ref)
    half, width = own_ref.shape[1], keep_ref.shape[2]

    def put(k, part):
        frames_ref[:, k * half : (k + 1) * half] = halves[part][...]

    put(2, 0)
    for k in range(2):
        for part in range(3 - k):
            pl.when(jnp.minimum(t, 2 - k) == part)(functools.partial(put, k, part))
    frames = frames_ref[...]
    spans = ((0, 5), (0, 6), (1, 6))
    count = 10
    even, odd = [None] * count, [None] * count
    for i in range(3):
        lo, hi = spans[i]
        sums = []
        for j in range(3):
            taps = wide_ref[i * 3 + j].reshape(3 * half, width)
            sums.append(jnp.dot(frames[lo * PITCH : hi * PITCH], taps, preferred_element_type=F32))
        at_even = down(sums[0]) + sums[1] + sums[2]
        at_odd = sums[0] + sums[1] + up(sums[2])
        for r in range(count):
            n = (r + 1) // 2 if i == 1 else r // 2
            at = slice(n * PITCH, (n + 1) * PITCH)
            even[r] = at_even[at] if even[r] is None else even[r] + at_even[at]
            odd[r] = at_odd[at] if odd[r] is None else odd[r] + at_odd[at]
    for p, rows in enumerate((even, odd)):
        for r in range(count):
            sum_ref[p, r * PITCH : (r + 1) * PITCH] = rows[r]
    step = 4 * PITCH
    size = keep_ref.shape[1]
    keep_ref[...] = sum_ref[:, pl.ds(pl.multiple_of(c * step, step), size), :]
    send_ref[...] = sum_ref[:, pl.ds(pl.multiple_of((1 - c) * step, step), size), :].astype(BF16)


def taps_of(k, acts, last_ref):
    size = 4 * PITCH
    parts = []
    for j in range(3):
        total = None
        for i in range(3):
            rows = slice(i * PITCH, i * PITCH + size)
            both = jnp.concatenate([acts[0][rows], acts[1][rows]], 0)
            part = jnp.dot(both, last_ref[k, i, j], preferred_element_type=F32)
            total = part if total is None else total + part
        parts.append(total)
    at_even = down(parts[0][size:]) + parts[1][:size] + parts[2][size:]
    at_odd = parts[0][:size] + parts[1][size:] + up(parts[2][:size])
    return jnp.concatenate([at_even, at_odd], 0)


def fine_kernel(across, at_ref, keep_ref, got_ref, last_ref, first_ref, second_ref, mid_ref, act_ref):
    t, strip, strips = at_ref[3], at_ref[4], at_ref[5]
    mid = (keep_ref[...] + got_ref[...].astype(F32)).astype(BF16)
    shape = mid.shape[1:]
    row = lax.broadcasted_iota(jnp.int32, shape, 0) // PITCH
    keep = column_mask(shape, 0, across)
    keep = keep & ((row > 0) | (strip > 0)) & ((row < 5) | (strip < strips - 1))
    acts = [jnp.where(keep, silu(mid[p].astype(F32)), 0.0).astype(BF16) for p in range(2)]
    for p in range(2):
        act_ref[p] = acts[p]
        mid_ref[p * 4 * PITCH : (p + 1) * 4 * PITCH] = mid[p, PITCH : 5 * PITCH]
    sums = [taps_of(k, acts, last_ref) for k in range(2)]
    first_ref[...] = jnp.where(t == 0, sums[0] + sums[1], sums[1]).astype(BF16)
    second_ref[...] = sums[0].astype(BF16)


def own_kernel(at_ref, mid_ref, act_ref, last_ref, first_ref, own_ref):
    acts = [act_ref[p] for p in range(2)]
    own = mid_ref[...].astype(F32) + taps_of(2, acts, last_ref)
    late = first_ref[...].astype(F32)
    own_ref[...] = own + jnp.where(at_ref[3] == 0, late, jnp.zeros(late.shape, F32))


def last_kernel(across, at_ref, own_ref, first_ref, second_ref, out_ref, order_ref):
    t = at_ref[3]
    zero = jnp.zeros(own_ref.shape, F32)
    total = (
        own_ref[...]
        + jnp.where(t >= 1, first_ref[...].astype(F32), zero)
        + jnp.where(t >= 2, second_ref[...].astype(F32), zero)
    )
    for parity in range(2):
        for h in range(4):
            at = (parity * 4 + h) * PITCH
            for half in range(2):
                order_ref[half, pl.ds(4 * parity + h, PITCH, stride=8), :] = total[
                    at : at + PITCH, 128 * half : 128 * half + 128
                ]
    for half in range(2):
        out_ref[:, 128 * half : 128 * half + 128] = order_ref[half, : 4 * across * 2].astype(BF16)


def turned(block, axis, distance):
    count = lax.axis_size(axis)
    return lax.ppermute(block, axis, [(i, (i + distance) % count) for i in range(count)])


def on_device(features, weight_one, weight_two, weight_three):
    own_block = features[0]
    height, across, shard = own_block.shape
    channels = weight_one.shape[3]
    cells = height * PITCH
    tp = ("z", "x", "c")
    at = jnp.stack(
        [lax.axis_index(a) for a in ("z", "x", "c", "tm")] + [lax.axis_index(tp), lax.axis_size(tp)]
    ).astype(jnp.int32)
    kernel = jnp.transpose(weight_one, (0, 1, 2, 4, 3)).reshape(27 * shard, channels)
    small = jax.ShapeDtypeStruct((shard, cells), BF16)
    field, act_in, slices = call(
        pack_kernel,
        (small, small, jax.ShapeDtypeStruct((4, 27 * shard, channels // 4), BF16)),
        tuple(pltpu.with_memory_space_constraint(a, pltpu.HBM) for a in (jnp.transpose(own_block, (1, 2, 0)), kernel)),
        (
            pltpu.VMEM((across, shard, height), BF16),
            pltpu.VMEM((PITCH * shard, LANES), F32),
            pltpu.VMEM((cells // LANES * shard, LANES), F32),
            pltpu.SemaphoreType.DMA((5,)),
        ),
        [HBM, HBM],
    )
    frames = jnp.concatenate([act_in, turned(act_in, "tm", 1), turned(act_in, "tm", 2)], 0)
    slices = lax.all_to_all(slices, "z", 0, 0, tiled=True)
    blocks = []
    for d in range(4):
        block = turned(frames, "x", d) if d else frames
        blocks += [block, turned(block, "c", 1)]
    cut = call(
        coarse_kernel,
        jax.ShapeDtypeStruct((16, 6 * shard, LANES), BF16),
        (at, field, slices, *blocks),
        (
            pltpu.VMEM((3 * channels // 4, cells + 2 * LANES), BF16),
            pltpu.VMEM((3, 12 * shard, 3 * channels // 4), BF16),
            pltpu.VMEM((4 * shard, cells + 2 * LANES), F32),
        ),
    )
    parts = lax.all_to_all(cut, ("z", "x"), 0, 0, tiled=True)
    own = pl.pallas_call(
        functools.partial(strip_kernel, across),
        out_shape=jax.ShapeDtypeStruct((6 * PITCH, channels // 2), BF16),
        scratch_shapes=[pltpu.VMEM((channels // 2, 2 * LANES), F32)],
        compiler_params=pltpu.CompilerParams(vmem_limit_bytes=LIMIT),
    )(parts)
    width = weight_two.shape[4]
    source = weight_two.reshape(3, 3, 3, -1, 2, shard, width)
    wide = call(
        stage_kernel,
        jax.ShapeDtypeStruct((9, 3, channels // 2 // shard, shard, width), BF16),
        (at, pltpu.with_memory_space_constraint(source, pltpu.HBM), own),
        (pltpu.SemaphoreType.DMA((9,)),),
        [SMEM, HBM, pl.BlockSpec(memory_space=pl.ANY)],
    )
    rows = 6 * PITCH
    keep, send = call(
        wide_kernel,
        (jax.ShapeDtypeStruct((2, rows, width), F32), jax.ShapeDtypeStruct((2, rows, width), BF16)),
        (at, own, turned(own, "tm", 1), turned(own, "tm", 2), wide),
        (pltpu.VMEM((rows, 3 * channels // 2), BF16), pltpu.VMEM((2, 10 * PITCH, width), F32)),
    )
    small = jax.ShapeDtypeStruct((8 * PITCH, width), BF16)
    first, second, mid, act = call(
        functools.partial(fine_kernel, across),
        (small, small, small, jax.ShapeDtypeStruct((2, rows, width), BF16)),
        (at, keep, turned(send, "c", 1), weight_three),
    )
    own = call(
        own_kernel,
        jax.ShapeDtypeStruct((8 * PITCH, width), F32),
        (at, mid, act, weight_three, first),
    )
    decoded = call(
        functools.partial(last_kernel, across),
        jax.ShapeDtypeStruct((8 * across, width), BF16),
        (at, own, turned(first, "tm", 1), turned(second, "tm", 2)),
        (pltpu.VMEM((2, 8 * PITCH, 128), F32),),
    )
    return jnp.transpose(decoded.reshape(2 * across, 4, width), (1, 0, 2))[None]


def solution(mesh):
    grid = Mesh(mesh.devices.reshape(mesh.shape["tm"], 4, 4, 2), ("tm", "z", "x", "c"))
    tp = ("z", "x", "c")
    return jax.shard_map(
        on_device,
        mesh=grid,
        in_specs=(P("tm", None, None, tp), P(None, None, None, None, tp), P(), P()),
        out_specs=P("tm", tp, None, None),
        check_vma=False,
    )
```

```python
import functools

import jax
import jax.numpy as jnp
from jax import lax
from jax.experimental import pallas as pl
from jax.experimental.pallas import tpu as pltpu
from jax.sharding import Mesh, PartitionSpec as P

PITCH = 32
LANES = 128
QUARTERS = 4
BF16 = jnp.bfloat16
F32 = jnp.float32
SMEM = pl.BlockSpec(memory_space=pltpu.SMEM)
HBM = pl.BlockSpec(memory_space=pltpu.HBM)
VMEM = pl.BlockSpec(memory_space=pltpu.VMEM)
LIMIT = 20 * 2**20


def call(kernel, out_shape, operands, scratch=(), specs=None):
    specs = specs or [SMEM] + [VMEM] * (len(operands) - 1)
    return pl.pallas_call(
        kernel,
        out_shape=out_shape,
        in_specs=specs,
        out_specs=jax.tree.map(lambda _: VMEM, out_shape),
        scratch_shapes=scratch,
        compiler_params=pltpu.CompilerParams(vmem_limit_bytes=LIMIT),
    )(*operands)


def silu(v):
    return v / (1.0 + jnp.exp(-v))


def column_mask(shape, axis, across):
    return lax.rem(lax.broadcasted_iota(jnp.int32, shape, axis), PITCH) < across


def before(block):
    lane = lax.broadcasted_iota(jnp.int32, block.shape, 1)
    return jnp.where(lane >= PITCH, pltpu.roll(block, PITCH, 1), 0.0)


def after(block):
    lane = lax.broadcasted_iota(jnp.int32, block.shape, 1)
    return jnp.where(lane < LANES - PITCH, pltpu.roll(block, LANES - PITCH, 1), 0.0)


def pack_kernel(field_ref, weight_ref, packed_ref, act_ref, slices_ref, raw_ref, columns_ref, rows_ref, sems):
    across, shard, height = field_ref.shape
    deep = height // QUARTERS
    load = pltpu.make_async_copy(field_ref, raw_ref, sems.at[4])
    load.start()
    width = weight_ref.shape[1] // 4
    copies = []
    for d in range(4):
        source = weight_ref.at[:, d * width : (d + 1) * width]
        copies.append(pltpu.make_async_copy(source, slices_ref.at[d], sems.at[d]))
        copies[d].start()
    columns_ref[...] = jnp.zeros(columns_ref.shape, F32)
    load.wait()
    columns_ref[: across * shard, :height] = raw_ref[...].astype(F32).reshape(across * shard, height)
    for c in range(shard):
        cells = columns_ref[pl.ds(c, PITCH, stride=shard), :].T
        quarters = [cells[q * deep : (q + 1) * deep] for q in range(QUARTERS)]
        rows_ref[pl.ds(c, deep, stride=shard), :] = jnp.concatenate(quarters, 1)
    for v in range(deep):
        values = rows_ref[v * shard : (v + 1) * shard, :]
        packed_ref[:, v * LANES : (v + 1) * LANES] = values.astype(BF16)
        act_ref[:, v * LANES : (v + 1) * LANES] = silu(values).astype(BF16)
    for copy in copies:
        copy.wait()


def coarse_kernel(at_ref, field_ref, slices_ref, *refs):
    blocks, (out_ref, all_ref, taps_ref, sum_ref) = refs[:8], refs[8:]
    shard, cells = field_ref.shape
    deep = cells // LANES
    group = 8 * shard
    wide = 4 * shard
    z, x, c, t = at_ref[0], at_ref[1], at_ref[2], at_ref[3]
    for n, block in enumerate(blocks):
        x_from = lax.rem(x + 4 - n // 2, 4)
        c_from = c if n % 2 == 0 else 1 - c
        base = (x_from * 2 + c_from) * shard
        for k in range(3):
            part = pl.multiple_of(jnp.minimum(t, 2 - k) * shard, shard)
            all_ref[pl.ds(pl.multiple_of(k * group + base, shard), shard), LANES : LANES + cells] = block[
                pl.ds(part, shard), :
            ]
    first, last = all_ref[:, LANES : 2 * LANES], all_ref[:, cells : cells + LANES]
    all_ref[:, :LANES] = before(last.astype(F32)).astype(BF16)
    all_ref[:, LANES + cells :] = after(first.astype(F32)).astype(BF16)
    for d in range(4):
        for k in range(3):
            for i in range(3):
                for j in range(3):
                    tap = (k * 3 + i) * 3 + j
                    to = j * wide + d * shard
                    at = (i * 3 + k) * group
                    taps_ref[to : to + shard, at : at + group] = slices_ref[d, tap * shard : (tap + 1) * shard, :]
    span = 4 * LANES
    for n in range(cells // span):
        shifted = [all_ref[:, i * LANES + n * span : i * LANES + (n + 1) * span] for i in range(3)]
        total = jnp.dot(taps_ref[...], jnp.concatenate(shifted, 0), preferred_element_type=F32)
        for v in range(4):
            left, here, right = (total[j * wide : (j + 1) * wide, v * LANES : (v + 1) * LANES] for j in range(3))
            lo = LANES + n * span + v * LANES
            sum_ref[:, lo : lo + LANES] = pltpu.roll(left, 1, 1) + here + pltpu.roll(right, LANES - 1, 1)
    own = pl.ds(pl.multiple_of(z * shard, shard), shard)
    sum_ref[own, LANES : LANES + cells] = sum_ref[own, LANES : LANES + cells] + field_ref[...].astype(F32)
    sum_ref[:, :LANES] = before(sum_ref[:, cells : cells + LANES])
    sum_ref[:, LANES + cells :] = after(sum_ref[:, LANES : 2 * LANES])
    at = lax.broadcasted_iota(jnp.int32, (wide, LANES), 1) // PITCH
    half = wide // 2

    def placed(pieces, q):
        moved = [pltpu.roll(p, (r - q) % 4 * PITCH, 1) if r != q else p for r, p in enumerate(pieces)]
        to = at[: pieces[0].shape[0]]
        return jnp.where(to < 2, jnp.where(to < 1, moved[0], moved[1]), jnp.where(to < 3, moved[2], moved[3]))

    for m in range(deep // 4):
        rows = [sum_ref[:, (4 * m + r) * LANES : (4 * m + r + 1) * LANES] for r in range(6)]
        rest = [rows[4][:half], rows[5][:half], rows[4][half:], rows[5][half:]]
        for q in range(QUARTERS):
            out_ref[q * (deep // 4) + m, :wide] = placed(rows[:4], q).astype(BF16)
            out_ref[q * (deep // 4) + m, wide:] = placed(rest, q).astype(BF16)


def strip_kernel(across, parts_ref, out_ref, order_ref):
    wide = parts_ref.shape[1] * 2 // 3
    shard = wide // 4
    order_ref[:, LANES:] = jnp.zeros((order_ref.shape[0], LANES), F32)
    for n in range(4):
        total = None
        for z in range(4):
            part = parts_ref[z * 4 + n].astype(F32)
            total = part if total is None else total + part
        act = silu(total.astype(BF16).astype(F32))
        act = jnp.where(column_mask(act.shape, 1, across), act, 0.0)
        rest = [act[wide:], pltpu.roll(act[wide:], LANES // 2, 1)]
        for z in range(4):
            to = slice((z * 4 + n) * shard, (z * 4 + n + 1) * shard)
            order_ref[to, :LANES] = act[z * shard : (z + 1) * shard]
            order_ref[to, LANES : LANES + LANES // 2] = rest[z // 2][z % 2 * shard : (z % 2 + 1) * shard, : LANES // 2]
    out_ref[...] = order_ref[...].T[: out_ref.shape[0]].astype(BF16)


def stage_kernel(at_ref, weight_ref, tie_ref, out_ref, sems):
    c = at_ref[2]
    copies = []
    for n in range(9):
        copies.append(pltpu.make_async_copy(weight_ref.at[:, n // 3, n % 3, :, c], out_ref.at[n], sems.at[n]))
        copies[n].start()
    for copy in copies:
        copy.wait()


def down(v):
    return pltpu.roll(v, 1, 0)


def up(v):
    return pltpu.roll(v, v.shape[0] - 1, 0)


def wide_kernel(at_ref, own_ref, first_ref, second_ref, wide_ref, keep_ref, send_ref, frames_ref, sum_ref):
    c, t = at_ref[2], at_ref[3]
    halves = (own_ref, first_ref, second_ref)
    half, width = own_ref.shape[1], keep_ref.shape[2]

    def put(k, part):
        frames_ref[:, k * half : (k + 1) * half] = halves[part][...]

    put(2, 0)
    for k in range(2):
        for part in range(3 - k):
            pl.when(jnp.minimum(t, 2 - k) == part)(functools.partial(put, k, part))
    frames = frames_ref[...]
    spans = ((0, 5), (0, 6), (1, 6))
    count = 10
    even, odd = [None] * count, [None] * count
    for i in range(3):
        lo, hi = spans[i]
        sums = []
        for j in range(3):
            taps = wide_ref[i * 3 + j].reshape(3 * half, width)
            sums.append(jnp.dot(frames[lo * PITCH : hi * PITCH], taps, preferred_element_type=F32))
        at_even = down(sums[0]) + sums[1] + sums[2]
        at_odd = sums[0] + sums[1] + up(sums[2])
        for r in range(count):
            n = (r + 1) // 2 if i == 1 else r // 2
            at = slice(n * PITCH, (n + 1) * PITCH)
            even[r] = at_even[at] if even[r] is None else even[r] + at_even[at]
            odd[r] = at_odd[at] if odd[r] is None else odd[r] + at_odd[at]
    for p, rows in enumerate((even, odd)):
        for r in range(count):
            sum_ref[p, r * PITCH : (r + 1) * PITCH] = rows[r]
    step = 4 * PITCH
    size = keep_ref.shape[1]
    keep_ref[...] = sum_ref[:, pl.ds(pl.multiple_of(c * step, step), size), :]
    send_ref[...] = sum_ref[:, pl.ds(pl.multiple_of((1 - c) * step, step), size), :].astype(BF16)


def taps_of(k, acts, last_ref):
    size = 4 * PITCH
    parts = []
    for j in range(3):
        total = None
        for i in range(3):
            rows = slice(i * PITCH, i * PITCH + size)
            both = jnp.concatenate([acts[0][rows], acts[1][rows]], 0)
            part = jnp.dot(both, last_ref[k, i, j], preferred_element_type=F32)
            total = part if total is None else total + part
        parts.append(total)
    at_even = down(parts[0][size:]) + parts[1][:size] + parts[2][size:]
    at_odd = parts[0][:size] + parts[1][size:] + up(parts[2][:size])
    return jnp.concatenate([at_even, at_odd], 0)


def fine_kernel(across, at_ref, keep_ref, got_ref, last_ref, first_ref, second_ref, mid_ref, act_ref):
    t, strip, strips = at_ref[3], at_ref[4], at_ref[5]
    mid = (keep_ref[...] + got_ref[...].astype(F32)).astype(BF16)
    shape = mid.shape[1:]
    row = lax.broadcasted_iota(jnp.int32, shape, 0) // PITCH
    keep = column_mask(shape, 0, across)
    keep = keep & ((row > 0) | (strip > 0)) & ((row < 5) | (strip < strips - 1))
    acts = [jnp.where(keep, silu(mid[p].astype(F32)), 0.0).astype(BF16) for p in range(2)]
    for p in range(2):
        act_ref[p] = acts[p]
        mid_ref[p * 4 * PITCH : (p + 1) * 4 * PITCH] = mid[p, PITCH : 5 * PITCH]
    sums = [taps_of(k, acts, last_ref) for k in range(2)]
    first_ref[...] = jnp.where(t == 0, sums[0] + sums[1], sums[1]).astype(BF16)
    second_ref[...] = sums[0].astype(BF16)


def own_kernel(at_ref, mid_ref, act_ref, last_ref, first_ref, own_ref):
    acts = [act_ref[p] for p in range(2)]
    own = mid_ref[...].astype(F32) + taps_of(2, acts, last_ref)
    late = first_ref[...].astype(F32)
    own_ref[...] = own + jnp.where(at_ref[3] == 0, late, jnp.zeros(late.shape, F32))


def last_kernel(across, at_ref, own_ref, first_ref, second_ref, out_ref, order_ref):
    t = at_ref[3]
    zero = jnp.zeros(own_ref.shape, F32)
    total = (
        own_ref[...]
        + jnp.where(t >= 1, first_ref[...].astype(F32), zero)
        + jnp.where(t >= 2, second_ref[...].astype(F32), zero)
    )
    for parity in range(2):
        for h in range(4):
            at = (parity * 4 + h) * PITCH
            for half in range(2):
                order_ref[half, pl.ds(4 * parity + h, PITCH, stride=8), :] = total[
                    at : at + PITCH, 128 * half : 128 * half + 128
                ]
    for half in range(2):
        out_ref[:, 128 * half : 128 * half + 128] = order_ref[half, : 4 * across * 2].astype(BF16)


def turned(block, axis, distance):
    count = lax.axis_size(axis)
    return lax.ppermute(block, axis, [(i, (i + distance) % count) for i in range(count)])


def on_device(features, weight_one, weight_two, weight_three):
    own_block = features[0]
    height, across, shard = own_block.shape
    channels = weight_one.shape[3]
    cells = height * PITCH
    tp = ("z", "x", "c")
    at = jnp.stack(
        [lax.axis_index(a) for a in ("z", "x", "c", "tm")] + [lax.axis_index(tp), lax.axis_size(tp)]
    ).astype(jnp.int32)
    kernel = jnp.transpose(weight_one, (0, 1, 2, 4, 3)).reshape(27 * shard, channels)
    small = jax.ShapeDtypeStruct((shard, cells), BF16)
    field, act_in, slices = call(
        pack_kernel,
        (small, small, jax.ShapeDtypeStruct((4, 27 * shard, channels // 4), BF16)),
        tuple(pltpu.with_memory_space_constraint(a, pltpu.HBM) for a in (jnp.transpose(own_block, (1, 2, 0)), kernel)),
        (
            pltpu.VMEM((across, shard, height), BF16),
            pltpu.VMEM((PITCH * shard, LANES), F32),
            pltpu.VMEM((cells // LANES * shard, LANES), F32),
            pltpu.SemaphoreType.DMA((5,)),
        ),
        [HBM, HBM],
    )
    frames = jnp.concatenate([act_in, turned(act_in, "tm", 1), turned(act_in, "tm", 2)], 0)
    slices = lax.all_to_all(slices, "z", 0, 0, tiled=True)
    blocks = []
    for d in range(4):
        block = turned(frames, "x", d) if d else frames
        blocks += [block, turned(block, "c", 1)]
    cut = call(
        coarse_kernel,
        jax.ShapeDtypeStruct((16, 6 * shard, LANES), BF16),
        (at, field, slices, *blocks),
        (
            pltpu.VMEM((3 * channels // 4, cells + 2 * LANES), BF16),
            pltpu.VMEM((12 * shard, 9 * channels // 4), BF16),
            pltpu.VMEM((4 * shard, cells + 2 * LANES), F32),
        ),
    )
    parts = lax.all_to_all(cut, ("z", "x"), 0, 0, tiled=True)
    own = pl.pallas_call(
        functools.partial(strip_kernel, across),
        out_shape=jax.ShapeDtypeStruct((6 * PITCH, channels // 2), BF16),
        scratch_shapes=[pltpu.VMEM((channels // 2, 2 * LANES), F32)],
        compiler_params=pltpu.CompilerParams(vmem_limit_bytes=LIMIT),
    )(parts)
    width = weight_two.shape[4]
    source = weight_two.reshape(3, 3, 3, -1, 2, shard, width)
    wide = call(
        stage_kernel,
        jax.ShapeDtypeStruct((9, 3, channels // 2 // shard, shard, width), BF16),
        (at, pltpu.with_memory_space_constraint(source, pltpu.HBM), own),
        (pltpu.SemaphoreType.DMA((9,)),),
        [SMEM, HBM, pl.BlockSpec(memory_space=pl.ANY)],
    )
    rows = 6 * PITCH
    keep, send = call(
        wide_kernel,
        (jax.ShapeDtypeStruct((2, rows, width), F32), jax.ShapeDtypeStruct((2, rows, width), BF16)),
        (at, own, turned(own, "tm", 1), turned(own, "tm", 2), wide),
        (pltpu.VMEM((rows, 3 * channels // 2), BF16), pltpu.VMEM((2, 10 * PITCH, width), F32)),
    )
    small = jax.ShapeDtypeStruct((8 * PITCH, width), BF16)
    first, second, mid, act = call(
        functools.partial(fine_kernel, across),
        (small, small, small, jax.ShapeDtypeStruct((2, rows, width), BF16)),
        (at, keep, turned(send, "c", 1), weight_three),
    )
    own = call(
        own_kernel,
        jax.ShapeDtypeStruct((8 * PITCH, width), F32),
        (at, mid, act, weight_three, first),
    )
    decoded = call(
        functools.partial(last_kernel, across),
        jax.ShapeDtypeStruct((8 * across, width), BF16),
        (at, own, turned(first, "tm", 1), turned(second, "tm", 2)),
        (pltpu.VMEM((2, 8 * PITCH, 128), F32),),
    )
    return jnp.transpose(decoded.reshape(2 * across, 4, width), (1, 0, 2))[None]


def solution(mesh):
    grid = Mesh(mesh.devices.reshape(mesh.shape["tm"], 4, 4, 2), ("tm", "z", "x", "c"))
    tp = ("z", "x", "c")
    return jax.shard_map(
        on_device,
        mesh=grid,
        in_specs=(P("tm", None, None, tp), P(None, None, None, None, tp), P(), P()),
        out_specs=P("tm", tp, None, None),
        check_vma=False,
    )
```

```python
import functools

import jax
import jax.numpy as jnp
from jax import lax
from jax.experimental import pallas as pl
from jax.experimental.pallas import tpu as pltpu
from jax.sharding import Mesh, PartitionSpec as P

PITCH = 32
LANES = 128
QUARTERS = 4
BF16 = jnp.bfloat16
F32 = jnp.float32
HBM = pl.BlockSpec(memory_space=pltpu.HBM)
VMEM = pl.BlockSpec(memory_space=pltpu.VMEM)
LIMIT = 20 * 2**20


def where_and(kernel, *refs):
    place = [lax.axis_index(a) for a in ("z", "x", "c", "tm")]
    z, x, c = place[:3]
    count = [lax.axis_size(a) for a in ("z", "x", "c")]
    strip = (z * count[1] + x) * count[2] + c
    kernel([*place, strip, count[0] * count[1] * count[2]], *refs)


def call(kernel, out_shape, operands, scratch=(), specs=None):
    specs = specs or [VMEM] * len(operands)
    return pl.pallas_call(
        functools.partial(where_and, kernel),
        out_shape=out_shape,
        in_specs=specs,
        out_specs=jax.tree.map(lambda _: VMEM, out_shape),
        scratch_shapes=scratch,
        compiler_params=pltpu.CompilerParams(vmem_limit_bytes=LIMIT),
    )(*operands)


def silu(v):
    return v / (1.0 + jnp.exp(-v))


def column_mask(shape, axis, across):
    return lax.rem(lax.broadcasted_iota(jnp.int32, shape, axis), PITCH) < across


def before(block):
    lane = lax.broadcasted_iota(jnp.int32, block.shape, 1)
    return jnp.where(lane >= PITCH, pltpu.roll(block, PITCH, 1), 0.0)


def after(block):
    lane = lax.broadcasted_iota(jnp.int32, block.shape, 1)
    return jnp.where(lane < LANES - PITCH, pltpu.roll(block, LANES - PITCH, 1), 0.0)


def pack_kernel(place, field_ref, weight_ref, packed_ref, act_ref, slices_ref, raw_ref, columns_ref, rows_ref, sems):
    across, shard, height = field_ref.shape
    deep = height // QUARTERS
    load = pltpu.make_async_copy(field_ref, raw_ref, sems.at[4])
    load.start()
    width = weight_ref.shape[1] // 4
    copies = []
    for d in range(4):
        source = weight_ref.at[:, d * width : (d + 1) * width]
        copies.append(pltpu.make_async_copy(source, slices_ref.at[d], sems.at[d]))
        copies[d].start()
    columns_ref[...] = jnp.zeros(columns_ref.shape, F32)
    load.wait()
    columns_ref[: across * shard, :height] = raw_ref[...].astype(F32).reshape(across * shard, height)
    for c in range(shard):
        cells = columns_ref[pl.ds(c, PITCH, stride=shard), :].T
        quarters = [cells[q * deep : (q + 1) * deep] for q in range(QUARTERS)]
        rows_ref[pl.ds(c, deep, stride=shard), :] = jnp.concatenate(quarters, 1)
    for v in range(deep):
        values = rows_ref[v * shard : (v + 1) * shard, :]
        packed_ref[:, v * LANES : (v + 1) * LANES] = values.astype(BF16)
        act_ref[:, v * LANES : (v + 1) * LANES] = silu(values).astype(BF16)
    for copy in copies:
        copy.wait()


def coarse_kernel(place, field_ref, slices_ref, *refs):
    blocks, (out_ref, all_ref, taps_ref, sum_ref) = refs[:8], refs[8:]
    shard, cells = field_ref.shape
    deep = cells // LANES
    group = 8 * shard
    wide = 4 * shard
    z, x, c, t = place[0], place[1], place[2], place[3]
    for n, block in enumerate(blocks):
        x_from = lax.rem(x + 4 - n // 2, 4)
        c_from = c if n % 2 == 0 else 1 - c
        base = (x_from * 2 + c_from) * shard
        for k in range(3):
            part = pl.multiple_of(jnp.minimum(t, 2 - k) * shard, shard)
            all_ref[pl.ds(pl.multiple_of(k * group + base, shard), shard), LANES : LANES + cells] = block[
                pl.ds(part, shard), :
            ]
    first, last = all_ref[:, LANES : 2 * LANES], all_ref[:, cells : cells + LANES]
    all_ref[:, :LANES] = before(last.astype(F32)).astype(BF16)
    all_ref[:, LANES + cells :] = after(first.astype(F32)).astype(BF16)
    for d in range(4):
        for k in range(3):
            for i in range(3):
                for j in range(3):
                    tap = (k * 3 + i) * 3 + j
                    to = j * wide + d * shard
                    at = (i * 3 + k) * group
                    taps_ref[to : to + shard, at : at + group] = slices_ref[d, tap * shard : (tap + 1) * shard, :]
    span = 4 * LANES
    for n in range(cells // span):
        shifted = [all_ref[:, i * LANES + n * span : i * LANES + (n + 1) * span] for i in range(3)]
        total = jnp.dot(taps_ref[...], jnp.concatenate(shifted, 0), preferred_element_type=F32)
        for v in range(4):
            left, here, right = (total[j * wide : (j + 1) * wide, v * LANES : (v + 1) * LANES] for j in range(3))
            lo = LANES + n * span + v * LANES
            sum_ref[:, lo : lo + LANES] = pltpu.roll(left, 1, 1) + here + pltpu.roll(right, LANES - 1, 1)
    own = pl.ds(pl.multiple_of(z * shard, shard), shard)
    sum_ref[own, LANES : LANES + cells] = sum_ref[own, LANES : LANES + cells] + field_ref[...].astype(F32)
    sum_ref[:, :LANES] = before(sum_ref[:, cells : cells + LANES])
    sum_ref[:, LANES + cells :] = after(sum_ref[:, LANES : 2 * LANES])
    at = lax.broadcasted_iota(jnp.int32, (wide, LANES), 1) // PITCH
    half = wide // 2

    def placed(pieces, q):
        moved = [pltpu.roll(p, (r - q) % 4 * PITCH, 1) if r != q else p for r, p in enumerate(pieces)]
        to = at[: pieces[0].shape[0]]
        return jnp.where(to < 2, jnp.where(to < 1, moved[0], moved[1]), jnp.where(to < 3, moved[2], moved[3]))

    for m in range(deep // 4):
        rows = [sum_ref[:, (4 * m + r) * LANES : (4 * m + r + 1) * LANES] for r in range(6)]
        rest = [rows[4][:half], rows[5][:half], rows[4][half:], rows[5][half:]]
        for q in range(QUARTERS):
            out_ref[q * (deep // 4) + m, :wide] = placed(rows[:4], q).astype(BF16)
            out_ref[q * (deep // 4) + m, wide:] = placed(rest, q).astype(BF16)


def strip_kernel(across, parts_ref, out_ref, order_ref):
    wide = parts_ref.shape[1] * 2 // 3
    shard = wide // 4
    order_ref[:, LANES:] = jnp.zeros((order_ref.shape[0], LANES), F32)
    for n in range(4):
        total = None
        for z in range(4):
            part = parts_ref[z * 4 + n].astype(F32)
            total = part if total is None else total + part
        act = silu(total.astype(BF16).astype(F32))
        act = jnp.where(column_mask(act.shape, 1, across), act, 0.0)
        rest = [act[wide:], pltpu.roll(act[wide:], LANES // 2, 1)]
        for z in range(4):
            to = slice((z * 4 + n) * shard, (z * 4 + n + 1) * shard)
            order_ref[to, :LANES] = act[z * shard : (z + 1) * shard]
            order_ref[to, LANES : LANES + LANES // 2] = rest[z // 2][z % 2 * shard : (z % 2 + 1) * shard, : LANES // 2]
    out_ref[...] = order_ref[...].T[: out_ref.shape[0]].astype(BF16)


def stage_kernel(place, weight_ref, tie_ref, out_ref, sems):
    c = place[2]
    copies = []
    for n in range(9):
        copies.append(pltpu.make_async_copy(weight_ref.at[:, n // 3, n % 3, :, c], out_ref.at[n], sems.at[n]))
        copies[n].start()
    for copy in copies:
        copy.wait()


def down(v):
    return pltpu.roll(v, 1, 0)


def up(v):
    return pltpu.roll(v, v.shape[0] - 1, 0)


def wide_kernel(place, own_ref, first_ref, second_ref, wide_ref, keep_ref, send_ref, frames_ref, sum_ref):
    c, t = place[2], place[3]
    halves = (own_ref, first_ref, second_ref)
    half, width = own_ref.shape[1], keep_ref.shape[2]

    def put(k, part):
        frames_ref[:, k * half : (k + 1) * half] = halves[part][...]

    put(2, 0)
    for k in range(2):
        for part in range(3 - k):
            pl.when(jnp.minimum(t, 2 - k) == part)(functools.partial(put, k, part))
    frames = frames_ref[...]
    spans = ((0, 5), (0, 6), (1, 6))
    count = 10
    even, odd = [None] * count, [None] * count
    for i in range(3):
        lo, hi = spans[i]
        sums = []
        for j in range(3):
            taps = wide_ref[i * 3 + j].reshape(3 * half, width)
            sums.append(jnp.dot(frames[lo * PITCH : hi * PITCH], taps, preferred_element_type=F32))
        at_even = down(sums[0]) + sums[1] + sums[2]
        at_odd = sums[0] + sums[1] + up(sums[2])
        for r in range(count):
            n = (r + 1) // 2 if i == 1 else r // 2
            at = slice(n * PITCH, (n + 1) * PITCH)
            even[r] = at_even[at] if even[r] is None else even[r] + at_even[at]
            odd[r] = at_odd[at] if odd[r] is None else odd[r] + at_odd[at]
    for p, rows in enumerate((even, odd)):
        for r in range(count):
            sum_ref[p, r * PITCH : (r + 1) * PITCH] = rows[r]
    step = 4 * PITCH
    size = keep_ref.shape[1]
    keep_ref[...] = sum_ref[:, pl.ds(pl.multiple_of(c * step, step), size), :]
    send_ref[...] = sum_ref[:, pl.ds(pl.multiple_of((1 - c) * step, step), size), :].astype(BF16)


def taps_of(k, acts, last_ref):
    size = 4 * PITCH
    parts = []
    for j in range(3):
        total = None
        for i in range(3):
            rows = slice(i * PITCH, i * PITCH + size)
            both = jnp.concatenate([acts[0][rows], acts[1][rows]], 0)
            part = jnp.dot(both, last_ref[k, i, j], preferred_element_type=F32)
            total = part if total is None else total + part
        parts.append(total)
    at_even = down(parts[0][size:]) + parts[1][:size] + parts[2][size:]
    at_odd = parts[0][:size] + parts[1][size:] + up(parts[2][:size])
    return jnp.concatenate([at_even, at_odd], 0)


def fine_kernel(across, place, keep_ref, got_ref, last_ref, first_ref, second_ref, mid_ref, act_ref):
    t, strip, strips = place[3], place[4], place[5]
    mid = (keep_ref[...] + got_ref[...].astype(F32)).astype(BF16)
    shape = mid.shape[1:]
    row = lax.broadcasted_iota(jnp.int32, shape, 0) // PITCH
    keep = column_mask(shape, 0, across)
    keep = keep & ((row > 0) | (strip > 0)) & ((row < 5) | (strip < strips - 1))
    acts = [jnp.where(keep, silu(mid[p].astype(F32)), 0.0).astype(BF16) for p in range(2)]
    for p in range(2):
        act_ref[p] = acts[p]
        mid_ref[p * 4 * PITCH : (p + 1) * 4 * PITCH] = mid[p, PITCH : 5 * PITCH]
    sums = [taps_of(k, acts, last_ref) for k in range(2)]
    first_ref[...] = jnp.where(t == 0, sums[0] + sums[1], sums[1]).astype(BF16)
    second_ref[...] = sums[0].astype(BF16)


def own_kernel(place, mid_ref, act_ref, last_ref, first_ref, own_ref):
    acts = [act_ref[p] for p in range(2)]
    own = mid_ref[...].astype(F32) + taps_of(2, acts, last_ref)
    late = first_ref[...].astype(F32)
    own_ref[...] = own + jnp.where(place[3] == 0, late, jnp.zeros(late.shape, F32))


def last_kernel(across, place, own_ref, first_ref, second_ref, out_ref, order_ref):
    t = place[3]
    zero = jnp.zeros(own_ref.shape, F32)
    total = (
        own_ref[...]
        + jnp.where(t >= 1, first_ref[...].astype(F32), zero)
        + jnp.where(t >= 2, second_ref[...].astype(F32), zero)
    )
    for parity in range(2):
        for h in range(4):
            at = (parity * 4 + h) * PITCH
            for half in range(2):
                order_ref[half, pl.ds(4 * parity + h, PITCH, stride=8), :] = total[
                    at : at + PITCH, 128 * half : 128 * half + 128
                ]
    for half in range(2):
        out_ref[:, 128 * half : 128 * half + 128] = order_ref[half, : 4 * across * 2].astype(BF16)


def turned(block, axis, distance):
    count = lax.axis_size(axis)
    return lax.ppermute(block, axis, [(i, (i + distance) % count) for i in range(count)])


def on_device(features, weight_one, weight_two, weight_three):
    own_block = features[0]
    height, across, shard = own_block.shape
    channels = weight_one.shape[3]
    cells = height * PITCH
    tp = ("z", "x", "c")
    kernel = jnp.transpose(weight_one, (0, 1, 2, 4, 3)).reshape(27 * shard, channels)
    small = jax.ShapeDtypeStruct((shard, cells), BF16)
    field, act_in, slices = call(
        pack_kernel,
        (small, small, jax.ShapeDtypeStruct((4, 27 * shard, channels // 4), BF16)),
        tuple(pltpu.with_memory_space_constraint(a, pltpu.HBM) for a in (jnp.transpose(own_block, (1, 2, 0)), kernel)),
        (
            pltpu.VMEM((across, shard, height), BF16),
            pltpu.VMEM((PITCH * shard, LANES), F32),
            pltpu.VMEM((cells // LANES * shard, LANES), F32),
            pltpu.SemaphoreType.DMA((5,)),
        ),
        [HBM, HBM],
    )
    frames = jnp.concatenate([act_in, turned(act_in, "tm", 1), turned(act_in, "tm", 2)], 0)
    slices = lax.all_to_all(slices, "z", 0, 0, tiled=True)
    blocks = []
    for d in range(4):
        block = turned(frames, "x", d) if d else frames
        blocks += [block, turned(block, "c", 1)]
    cut = call(
        coarse_kernel,
        jax.ShapeDtypeStruct((16, 6 * shard, LANES), BF16),
        (field, slices, *blocks),
        (
            pltpu.VMEM((3 * channels // 4, cells + 2 * LANES), BF16),
            pltpu.VMEM((12 * shard, 9 * channels // 4), BF16),
            pltpu.VMEM((4 * shard, cells + 2 * LANES), F32),
        ),
    )
    parts = lax.all_to_all(cut, ("z", "x"), 0, 0, tiled=True)
    own = pl.pallas_call(
        functools.partial(strip_kernel, across),
        out_shape=jax.ShapeDtypeStruct((6 * PITCH, channels // 2), BF16),
        scratch_shapes=[pltpu.VMEM((channels // 2, 2 * LANES), F32)],
        compiler_params=pltpu.CompilerParams(vmem_limit_bytes=LIMIT),
    )(parts)
    width = weight_two.shape[4]
    source = weight_two.reshape(3, 3, 3, -1, 2, shard, width)
    wide = call(
        stage_kernel,
        jax.ShapeDtypeStruct((9, 3, channels // 2 // shard, shard, width), BF16),
        (pltpu.with_memory_space_constraint(source, pltpu.HBM), own),
        (pltpu.SemaphoreType.DMA((9,)),),
        [HBM, pl.BlockSpec(memory_space=pl.ANY)],
    )
    rows = 6 * PITCH
    keep, send = call(
        wide_kernel,
        (jax.ShapeDtypeStruct((2, rows, width), F32), jax.ShapeDtypeStruct((2, rows, width), BF16)),
        (own, turned(own, "tm", 1), turned(own, "tm", 2), wide),
        (pltpu.VMEM((rows, 3 * channels // 2), BF16), pltpu.VMEM((2, 10 * PITCH, width), F32)),
    )
    small = jax.ShapeDtypeStruct((8 * PITCH, width), BF16)
    first, second, mid, act = call(
        functools.partial(fine_kernel, across),
        (small, small, small, jax.ShapeDtypeStruct((2, rows, width), BF16)),
        (keep, turned(send, "c", 1), weight_three),
    )
    own = call(
        own_kernel,
        jax.ShapeDtypeStruct((8 * PITCH, width), F32),
        (mid, act, weight_three, first),
    )
    decoded = call(
        functools.partial(last_kernel, across),
        jax.ShapeDtypeStruct((8 * across, width), BF16),
        (own, turned(first, "tm", 1), turned(second, "tm", 2)),
        (pltpu.VMEM((2, 8 * PITCH, 128), F32),),
    )
    return jnp.transpose(decoded.reshape(2 * across, 4, width), (1, 0, 2))[None]


def solution(mesh):
    grid = Mesh(mesh.devices.reshape(mesh.shape["tm"], 4, 4, 2), ("tm", "z", "x", "c"))
    tp = ("z", "x", "c")
    return jax.shard_map(
        on_device,
        mesh=grid,
        in_specs=(P("tm", None, None, tp), P(None, None, None, None, tp), P(), P()),
        out_specs=P("tm", tp, None, None),
        check_vma=False,
    )
```

```python
import functools

import jax
import jax.numpy as jnp
from jax import lax
from jax.experimental import pallas as pl
from jax.experimental.pallas import tpu as pltpu
from jax.sharding import Mesh, PartitionSpec as P

PITCH = 32
LANES = 128
QUARTERS = 4
BF16 = jnp.bfloat16
F32 = jnp.float32
HBM = pl.BlockSpec(memory_space=pltpu.HBM)
VMEM = pl.BlockSpec(memory_space=pltpu.VMEM)
LIMIT = 20 * 2**20


def where_and(kernel, *refs):
    place = [lax.axis_index(a) for a in ("z", "x", "c", "tm")]
    z, x, c = place[:3]
    count = [lax.axis_size(a) for a in ("z", "x", "c")]
    strip = (z * count[1] + x) * count[2] + c
    kernel([*place, strip, count[0] * count[1] * count[2]], *refs)


def call(kernel, out_shape, operands, scratch=(), specs=None):
    specs = specs or [VMEM] * len(operands)
    return pl.pallas_call(
        functools.partial(where_and, kernel),
        out_shape=out_shape,
        in_specs=specs,
        out_specs=jax.tree.map(lambda _: VMEM, out_shape),
        scratch_shapes=scratch,
        compiler_params=pltpu.CompilerParams(vmem_limit_bytes=LIMIT),
    )(*operands)


def silu(v):
    return v / (1.0 + jnp.exp(-v))


def column_mask(shape, axis, across):
    return lax.rem(lax.broadcasted_iota(jnp.int32, shape, axis), PITCH) < across


def before(block):
    lane = lax.broadcasted_iota(jnp.int32, block.shape, 1)
    return jnp.where(lane >= PITCH, pltpu.roll(block, PITCH, 1), 0.0)


def after(block):
    lane = lax.broadcasted_iota(jnp.int32, block.shape, 1)
    return jnp.where(lane < LANES - PITCH, pltpu.roll(block, LANES - PITCH, 1), 0.0)


def pack_kernel(place, field_ref, weight_ref, packed_ref, act_ref, slices_ref, raw_ref, columns_ref, rows_ref, sems):
    across, shard, height = field_ref.shape
    deep = height // QUARTERS
    load = pltpu.make_async_copy(field_ref, raw_ref, sems.at[4])
    load.start()
    width = weight_ref.shape[1] // 4
    copies = []
    for d in range(4):
        source = weight_ref.at[:, d * width : (d + 1) * width]
        copies.append(pltpu.make_async_copy(source, slices_ref.at[d], sems.at[d]))
        copies[d].start()
    columns_ref[...] = jnp.zeros(columns_ref.shape, F32)
    load.wait()
    columns_ref[: across * shard, :height] = raw_ref[...].astype(F32).reshape(across * shard, height)
    for c in range(shard):
        cells = columns_ref[pl.ds(c, PITCH, stride=shard), :].T
        quarters = [cells[q * deep : (q + 1) * deep] for q in range(QUARTERS)]
        rows_ref[pl.ds(c, deep, stride=shard), :] = jnp.concatenate(quarters, 1)
    for v in range(deep):
        values = rows_ref[v * shard : (v + 1) * shard, :]
        packed_ref[:, v * LANES : (v + 1) * LANES] = values.astype(BF16)
        act_ref[:, v * LANES : (v + 1) * LANES] = silu(values).astype(BF16)
    for copy in copies:
        copy.wait()


def coarse_kernel(place, field_ref, slices_ref, *refs):
    blocks, (out_ref, all_ref, taps_ref, sum_ref) = refs[:8], refs[8:]
    shard, cells = field_ref.shape
    deep = cells // LANES
    group = 8 * shard
    wide = 4 * shard
    z, x, c, t = place[0], place[1], place[2], place[3]
    for n, block in enumerate(blocks):
        x_from = lax.rem(x + 4 - n // 2, 4)
        c_from = c if n % 2 == 0 else 1 - c
        base = (x_from * 2 + c_from) * shard
        for k in range(3):
            part = pl.multiple_of(jnp.minimum(t, 2 - k) * shard, shard)
            all_ref[pl.ds(pl.multiple_of(k * group + base, shard), shard), LANES : LANES + cells] = block[
                pl.ds(part, shard), :
            ]
    first, last = all_ref[:, LANES : 2 * LANES], all_ref[:, cells : cells + LANES]
    all_ref[:, :LANES] = before(last.astype(F32)).astype(BF16)
    all_ref[:, LANES + cells :] = after(first.astype(F32)).astype(BF16)
    for d in range(4):
        for k in range(3):
            for i in range(3):
                for j in range(3):
                    tap = (k * 3 + i) * 3 + j
                    to = j * wide + d * shard
                    at = (i * 3 + k) * group
                    taps_ref[to : to + shard, at : at + group] = slices_ref[d, tap * shard : (tap + 1) * shard, :]
    span = 4 * LANES
    for n in range(cells // span):
        shifted = [all_ref[:, i * LANES + n * span : i * LANES + (n + 1) * span] for i in range(3)]
        total = jnp.dot(taps_ref[...], jnp.concatenate(shifted, 0), preferred_element_type=F32)
        for v in range(4):
            left, here, right = (total[j * wide : (j + 1) * wide, v * LANES : (v + 1) * LANES] for j in range(3))
            lo = LANES + n * span + v * LANES
            sum_ref[:, lo : lo + LANES] = pltpu.roll(left, 1, 1) + here + pltpu.roll(right, LANES - 1, 1)
    own = pl.ds(pl.multiple_of(z * shard, shard), shard)
    sum_ref[own, LANES : LANES + cells] = sum_ref[own, LANES : LANES + cells] + field_ref[...].astype(F32)
    sum_ref[:, :LANES] = before(sum_ref[:, cells : cells + LANES])
    sum_ref[:, LANES + cells :] = after(sum_ref[:, LANES : 2 * LANES])
    at = lax.broadcasted_iota(jnp.int32, (wide, LANES), 1) // PITCH
    half = wide // 2

    def placed(pieces, q):
        moved = [pltpu.roll(p, (r - q) % 4 * PITCH, 1) if r != q else p for r, p in enumerate(pieces)]
        to = at[: pieces[0].shape[0]]
        return jnp.where(to < 2, jnp.where(to < 1, moved[0], moved[1]), jnp.where(to < 3, moved[2], moved[3]))

    for m in range(deep // 4):
        rows = [sum_ref[:, (4 * m + r) * LANES : (4 * m + r + 1) * LANES] for r in range(6)]
        rest = [rows[4][:half], rows[5][:half], rows[4][half:], rows[5][half:]]
        for q in range(QUARTERS):
            out_ref[q * (deep // 4) + m, :wide] = placed(rows[:4], q).astype(BF16)
            out_ref[q * (deep // 4) + m, wide:] = placed(rest, q).astype(BF16)


def strip_kernel(across, parts_ref, out_ref, order_ref):
    wide = parts_ref.shape[1] * 2 // 3
    shard = wide // 4
    order_ref[:, LANES:] = jnp.zeros((order_ref.shape[0], LANES), F32)
    for n in range(4):
        total = None
        for z in range(4):
            part = parts_ref[z * 4 + n].astype(F32)
            total = part if total is None else total + part
        act = silu(total.astype(BF16).astype(F32))
        act = jnp.where(column_mask(act.shape, 1, across), act, 0.0)
        rest = [act[wide:], pltpu.roll(act[wide:], LANES // 2, 1)]
        for z in range(4):
            to = slice((z * 4 + n) * shard, (z * 4 + n + 1) * shard)
            order_ref[to, :LANES] = act[z * shard : (z + 1) * shard]
            order_ref[to, LANES : LANES + LANES // 2] = rest[z // 2][z % 2 * shard : (z % 2 + 1) * shard, : LANES // 2]
    out_ref[...] = order_ref[...].T[: out_ref.shape[0]].astype(BF16)


def stage_kernel(place, weight_ref, tie_ref, out_ref, sems):
    c = place[2]
    copies = []
    for n in range(9):
        copies.append(pltpu.make_async_copy(weight_ref.at[:, n // 3, n % 3, :, c], out_ref.at[n], sems.at[n]))
        copies[n].start()
    for copy in copies:
        copy.wait()


def down(v):
    return pltpu.roll(v, 1, 0)


def up(v):
    return pltpu.roll(v, v.shape[0] - 1, 0)


def wide_kernel(place, own_ref, first_ref, second_ref, wide_ref, keep_ref, send_ref, frames_ref, sum_ref):
    c, t = place[2], place[3]
    halves = (own_ref, first_ref, second_ref)
    half, width = own_ref.shape[1], keep_ref.shape[2]

    def put(k, part):
        frames_ref[:, k * half : (k + 1) * half] = halves[part][...]

    put(2, 0)
    for k in range(2):
        for part in range(3 - k):
            pl.when(jnp.minimum(t, 2 - k) == part)(functools.partial(put, k, part))
    frames = frames_ref[...]
    spans = ((0, 5), (0, 6), (1, 6))
    count = 10
    even, odd = [None] * count, [None] * count
    for i in range(3):
        lo, hi = spans[i]
        sums = []
        for j in range(3):
            taps = wide_ref[i * 3 + j].reshape(3 * half, width)
            sums.append(jnp.dot(frames[lo * PITCH : hi * PITCH], taps, preferred_element_type=F32))
        at_even = down(sums[0]) + sums[1] + sums[2]
        at_odd = sums[0] + sums[1] + up(sums[2])
        for r in range(count):
            n = (r + 1) // 2 if i == 1 else r // 2
            at = slice(n * PITCH, (n + 1) * PITCH)
            even[r] = at_even[at] if even[r] is None else even[r] + at_even[at]
            odd[r] = at_odd[at] if odd[r] is None else odd[r] + at_odd[at]
    for p, rows in enumerate((even, odd)):
        for r in range(count):
            sum_ref[p, r * PITCH : (r + 1) * PITCH] = rows[r]
    step = 4 * PITCH
    size = keep_ref.shape[1]
    keep_ref[...] = sum_ref[:, pl.ds(pl.multiple_of(c * step, step), size), :]
    send_ref[...] = sum_ref[:, pl.ds(pl.multiple_of((1 - c) * step, step), size), :].astype(BF16)


def taps_of(k, acts, last_ref):
    size = 4 * PITCH
    rows = [slice(i * PITCH, i * PITCH + size) for i in range(3)]
    both = jnp.concatenate([jnp.concatenate([acts[0][at], acts[1][at]], 0) for at in rows], 1)
    parts = []
    for j in range(3):
        taps = jnp.concatenate([last_ref[k, i, j] for i in range(3)], 0)
        parts.append(jnp.dot(both, taps, preferred_element_type=F32))
    at_even = down(parts[0][size:]) + parts[1][:size] + parts[2][size:]
    at_odd = parts[0][:size] + parts[1][size:] + up(parts[2][:size])
    return jnp.concatenate([at_even, at_odd], 0)


def fine_kernel(across, place, keep_ref, got_ref, last_ref, first_ref, second_ref, mid_ref, act_ref):
    t, strip, strips = place[3], place[4], place[5]
    mid = (keep_ref[...] + got_ref[...].astype(F32)).astype(BF16)
    shape = mid.shape[1:]
    row = lax.broadcasted_iota(jnp.int32, shape, 0) // PITCH
    keep = column_mask(shape, 0, across)
    keep = keep & ((row > 0) | (strip > 0)) & ((row < 5) | (strip < strips - 1))
    acts = [jnp.where(keep, silu(mid[p].astype(F32)), 0.0).astype(BF16) for p in range(2)]
    for p in range(2):
        act_ref[p] = acts[p]
        mid_ref[p * 4 * PITCH : (p + 1) * 4 * PITCH] = mid[p, PITCH : 5 * PITCH]
    sums = [taps_of(k, acts, last_ref) for k in range(2)]
    first_ref[...] = jnp.where(t == 0, sums[0] + sums[1], sums[1]).astype(BF16)
    second_ref[...] = sums[0].astype(BF16)


def own_kernel(place, mid_ref, act_ref, last_ref, first_ref, own_ref):
    acts = [act_ref[p] for p in range(2)]
    own = mid_ref[...].astype(F32) + taps_of(2, acts, last_ref)
    late = first_ref[...].astype(F32)
    own_ref[...] = own + jnp.where(place[3] == 0, late, jnp.zeros(late.shape, F32))


def last_kernel(across, place, own_ref, first_ref, second_ref, out_ref, order_ref):
    t = place[3]
    zero = jnp.zeros(own_ref.shape, F32)
    total = (
        own_ref[...]
        + jnp.where(t >= 1, first_ref[...].astype(F32), zero)
        + jnp.where(t >= 2, second_ref[...].astype(F32), zero)
    )
    for parity in range(2):
        for h in range(4):
            at = (parity * 4 + h) * PITCH
            for half in range(2):
                order_ref[half, pl.ds(4 * parity + h, PITCH, stride=8), :] = total[
                    at : at + PITCH, 128 * half : 128 * half + 128
                ]
    for half in range(2):
        out_ref[:, 128 * half : 128 * half + 128] = order_ref[half, : 4 * across * 2].astype(BF16)


def turned(block, axis, distance):
    count = lax.axis_size(axis)
    return lax.ppermute(block, axis, [(i, (i + distance) % count) for i in range(count)])


def on_device(features, weight_one, weight_two, weight_three):
    own_block = features[0]
    height, across, shard = own_block.shape
    channels = weight_one.shape[3]
    cells = height * PITCH
    tp = ("z", "x", "c")
    kernel = jnp.transpose(weight_one, (0, 1, 2, 4, 3)).reshape(27 * shard, channels)
    small = jax.ShapeDtypeStruct((shard, cells), BF16)
    field, act_in, slices = call(
        pack_kernel,
        (small, small, jax.ShapeDtypeStruct((4, 27 * shard, channels // 4), BF16)),
        tuple(pltpu.with_memory_space_constraint(a, pltpu.HBM) for a in (jnp.transpose(own_block, (1, 2, 0)), kernel)),
        (
            pltpu.VMEM((across, shard, height), BF16),
            pltpu.VMEM((PITCH * shard, LANES), F32),
            pltpu.VMEM((cells // LANES * shard, LANES), F32),
            pltpu.SemaphoreType.DMA((5,)),
        ),
        [HBM, HBM],
    )
    frames = jnp.concatenate([act_in, turned(act_in, "tm", 1), turned(act_in, "tm", 2)], 0)
    slices = lax.all_to_all(slices, "z", 0, 0, tiled=True)
    blocks = []
    for d in range(4):
        block = turned(frames, "x", d) if d else frames
        blocks += [block, turned(block, "c", 1)]
    cut = call(
        coarse_kernel,
        jax.ShapeDtypeStruct((16, 6 * shard, LANES), BF16),
        (field, slices, *blocks),
        (
            pltpu.VMEM((3 * channels // 4, cells + 2 * LANES), BF16),
            pltpu.VMEM((12 * shard, 9 * channels // 4), BF16),
            pltpu.VMEM((4 * shard, cells + 2 * LANES), F32),
        ),
    )
    parts = lax.all_to_all(cut, ("z", "x"), 0, 0, tiled=True)
    own = pl.pallas_call(
        functools.partial(strip_kernel, across),
        out_shape=jax.ShapeDtypeStruct((6 * PITCH, channels // 2), BF16),
        scratch_shapes=[pltpu.VMEM((channels // 2, 2 * LANES), F32)],
        compiler_params=pltpu.CompilerParams(vmem_limit_bytes=LIMIT),
    )(parts)
    width = weight_two.shape[4]
    source = weight_two.reshape(3, 3, 3, -1, 2, shard, width)
    wide = call(
        stage_kernel,
        jax.ShapeDtypeStruct((9, 3, channels // 2 // shard, shard, width), BF16),
        (pltpu.with_memory_space_constraint(source, pltpu.HBM), own),
        (pltpu.SemaphoreType.DMA((9,)),),
        [HBM, pl.BlockSpec(memory_space=pl.ANY)],
    )
    rows = 6 * PITCH
    keep, send = call(
        wide_kernel,
        (jax.ShapeDtypeStruct((2, rows, width), F32), jax.ShapeDtypeStruct((2, rows, width), BF16)),
        (own, turned(own, "tm", 1), turned(own, "tm", 2), wide),
        (pltpu.VMEM((rows, 3 * channels // 2), BF16), pltpu.VMEM((2, 10 * PITCH, width), F32)),
    )
    small = jax.ShapeDtypeStruct((8 * PITCH, width), BF16)
    first, second, mid, act = call(
        functools.partial(fine_kernel, across),
        (small, small, small, jax.ShapeDtypeStruct((2, rows, width), BF16)),
        (keep, turned(send, "c", 1), weight_three),
    )
    own = call(
        own_kernel,
        jax.ShapeDtypeStruct((8 * PITCH, width), F32),
        (mid, act, weight_three, first),
    )
    decoded = call(
        functools.partial(last_kernel, across),
        jax.ShapeDtypeStruct((8 * across, width), BF16),
        (own, turned(first, "tm", 1), turned(second, "tm", 2)),
        (pltpu.VMEM((2, 8 * PITCH, 128), F32),),
    )
    return jnp.transpose(decoded.reshape(2 * across, 4, width), (1, 0, 2))[None]


def solution(mesh):
    grid = Mesh(mesh.devices.reshape(mesh.shape["tm"], 4, 4, 2), ("tm", "z", "x", "c"))
    tp = ("z", "x", "c")
    return jax.shard_map(
        on_device,
        mesh=grid,
        in_specs=(P("tm", None, None, tp), P(None, None, None, None, tp), P(), P()),
        out_specs=P("tm", tp, None, None),
        check_vma=False,
    )
```

```python
import functools

import jax
import jax.numpy as jnp
from jax import lax
from jax.experimental import pallas as pl
from jax.experimental.pallas import tpu as pltpu
from jax.sharding import Mesh, PartitionSpec as P

PITCH = 32
LANES = 128
QUARTERS = 4
BF16 = jnp.bfloat16
F32 = jnp.float32
HBM = pl.BlockSpec(memory_space=pltpu.HBM)
VMEM = pl.BlockSpec(memory_space=pltpu.VMEM)
LIMIT = 20 * 2**20


def where_and(kernel, *refs):
    place = [lax.axis_index(a) for a in ("z", "x", "c", "tm")]
    z, x, c = place[:3]
    count = [lax.axis_size(a) for a in ("z", "x", "c")]
    strip = (z * count[1] + x) * count[2] + c
    kernel([*place, strip, count[0] * count[1] * count[2]], *refs)


def call(kernel, out_shape, operands, scratch=(), specs=None):
    specs = specs or [VMEM] * len(operands)
    return pl.pallas_call(
        functools.partial(where_and, kernel),
        out_shape=out_shape,
        in_specs=specs,
        out_specs=jax.tree.map(lambda _: VMEM, out_shape),
        scratch_shapes=scratch,
        compiler_params=pltpu.CompilerParams(vmem_limit_bytes=LIMIT),
    )(*operands)


def silu(v):
    return v / (1.0 + jnp.exp(-v))


def column_mask(shape, axis, across):
    return lax.rem(lax.broadcasted_iota(jnp.int32, shape, axis), PITCH) < across


def before(block):
    lane = lax.broadcasted_iota(jnp.int32, block.shape, 1)
    return jnp.where(lane >= PITCH, pltpu.roll(block, PITCH, 1), 0.0)


def after(block):
    lane = lax.broadcasted_iota(jnp.int32, block.shape, 1)
    return jnp.where(lane < LANES - PITCH, pltpu.roll(block, LANES - PITCH, 1), 0.0)


def pack_kernel(place, field_ref, weight_ref, packed_ref, act_ref, slices_ref, raw_ref, columns_ref, rows_ref, sems):
    across, shard, height = field_ref.shape
    deep = height // QUARTERS
    load = pltpu.make_async_copy(field_ref, raw_ref, sems.at[4])
    load.start()
    width = weight_ref.shape[1] // 4
    copies = []
    for d in range(4):
        source = weight_ref.at[:, d * width : (d + 1) * width]
        copies.append(pltpu.make_async_copy(source, slices_ref.at[d], sems.at[d]))
        copies[d].start()
    columns_ref[...] = jnp.zeros(columns_ref.shape, F32)
    load.wait()
    columns_ref[: across * shard, :height] = raw_ref[...].astype(F32).reshape(across * shard, height)
    for c in range(shard):
        cells = columns_ref[pl.ds(c, PITCH, stride=shard), :].T
        quarters = [cells[q * deep : (q + 1) * deep] for q in range(QUARTERS)]
        rows_ref[pl.ds(c, deep, stride=shard), :] = jnp.concatenate(quarters, 1)
    for v in range(deep):
        values = rows_ref[v * shard : (v + 1) * shard, :]
        packed_ref[:, v * LANES : (v + 1) * LANES] = values.astype(BF16)
        act_ref[:, v * LANES : (v + 1) * LANES] = silu(values).astype(BF16)
    for copy in copies:
        copy.wait()


def coarse_kernel(place, field_ref, slices_ref, *refs):
    blocks, (out_ref, all_ref, taps_ref, sum_ref) = refs[:8], refs[8:]
    shard, cells = field_ref.shape
    deep = cells // LANES
    group = 8 * shard
    wide = 4 * shard
    z, x, c, t = place[0], place[1], place[2], place[3]
    for n, block in enumerate(blocks):
        x_from = lax.rem(x + 4 - n // 2, 4)
        c_from = c if n % 2 == 0 else 1 - c
        base = (x_from * 2 + c_from) * shard
        for k in range(3):
            part = pl.multiple_of(jnp.minimum(t, 2 - k) * shard, shard)
            all_ref[pl.ds(pl.multiple_of(k * group + base, shard), shard), LANES : LANES + cells] = block[
                pl.ds(part, shard), :
            ]
    first, last = all_ref[:, LANES : 2 * LANES], all_ref[:, cells : cells + LANES]
    all_ref[:, :LANES] = before(last.astype(F32)).astype(BF16)
    all_ref[:, LANES + cells :] = after(first.astype(F32)).astype(BF16)
    for d in range(4):
        for k in range(3):
            for i in range(3):
                for j in range(3):
                    tap = (k * 3 + i) * 3 + j
                    to = j * wide + d * shard
                    at = (i * 3 + k) * group
                    taps_ref[to : to + shard, at : at + group] = slices_ref[d, tap * shard : (tap + 1) * shard, :]
    span = 4 * LANES
    for n in range(cells // span):
        shifted = [all_ref[:, i * LANES + n * span : i * LANES + (n + 1) * span] for i in range(3)]
        total = jnp.dot(taps_ref[...], jnp.concatenate(shifted, 0), preferred_element_type=F32)
        for v in range(4):
            left, here, right = (total[j * wide : (j + 1) * wide, v * LANES : (v + 1) * LANES] for j in range(3))
            lo = LANES + n * span + v * LANES
            sum_ref[:, lo : lo + LANES] = pltpu.roll(left, 1, 1) + here + pltpu.roll(right, LANES - 1, 1)
    own = pl.ds(pl.multiple_of(z * shard, shard), shard)
    sum_ref[own, LANES : LANES + cells] = sum_ref[own, LANES : LANES + cells] + field_ref[...].astype(F32)
    sum_ref[:, :LANES] = before(sum_ref[:, cells : cells + LANES])
    sum_ref[:, LANES + cells :] = after(sum_ref[:, LANES : 2 * LANES])
    at = lax.broadcasted_iota(jnp.int32, (wide, LANES), 1) // PITCH
    half = wide // 2

    def placed(pieces, q):
        moved = [pltpu.roll(p, (r - q) % 4 * PITCH, 1) if r != q else p for r, p in enumerate(pieces)]
        to = at[: pieces[0].shape[0]]
        return jnp.where(to < 2, jnp.where(to < 1, moved[0], moved[1]), jnp.where(to < 3, moved[2], moved[3]))

    for m in range(deep // 4):
        rows = [sum_ref[:, (4 * m + r) * LANES : (4 * m + r + 1) * LANES].astype(BF16) for r in range(6)]
        rest = [rows[4][:half], rows[5][:half], rows[4][half:], rows[5][half:]]
        for q in range(QUARTERS):
            out_ref[q * (deep // 4) + m, :wide] = placed(rows[:4], q)
            out_ref[q * (deep // 4) + m, wide:] = placed(rest, q)


def strip_kernel(across, parts_ref, out_ref, order_ref):
    wide = parts_ref.shape[1] * 2 // 3
    shard = wide // 4
    order_ref[:, LANES:] = jnp.zeros((order_ref.shape[0], LANES), F32)
    for n in range(4):
        total = None
        for z in range(4):
            part = parts_ref[z * 4 + n].astype(F32)
            total = part if total is None else total + part
        act = silu(total.astype(BF16).astype(F32))
        act = jnp.where(column_mask(act.shape, 1, across), act, 0.0)
        rest = [act[wide:], pltpu.roll(act[wide:], LANES // 2, 1)]
        for z in range(4):
            to = slice((z * 4 + n) * shard, (z * 4 + n + 1) * shard)
            order_ref[to, :LANES] = act[z * shard : (z + 1) * shard]
            order_ref[to, LANES : LANES + LANES // 2] = rest[z // 2][z % 2 * shard : (z % 2 + 1) * shard, : LANES // 2]
    out_ref[...] = order_ref[...].T[: out_ref.shape[0]].astype(BF16)


def stage_kernel(place, weight_ref, tie_ref, out_ref, sems):
    c = place[2]
    copies = []
    for n in range(9):
        copies.append(pltpu.make_async_copy(weight_ref.at[:, n // 3, n % 3, :, c], out_ref.at[n], sems.at[n]))
        copies[n].start()
    for copy in copies:
        copy.wait()


def down(v):
    return pltpu.roll(v, 1, 0)


def up(v):
    return pltpu.roll(v, v.shape[0] - 1, 0)


def wide_kernel(place, own_ref, first_ref, second_ref, wide_ref, keep_ref, send_ref, frames_ref, sum_ref):
    c, t = place[2], place[3]
    halves = (own_ref, first_ref, second_ref)
    half, width = own_ref.shape[1], keep_ref.shape[2]

    def put(k, part):
        frames_ref[:, k * half : (k + 1) * half] = halves[part][...]

    put(2, 0)
    for k in range(2):
        for part in range(3 - k):
            pl.when(jnp.minimum(t, 2 - k) == part)(functools.partial(put, k, part))
    frames = frames_ref[...]
    spans = ((0, 5), (0, 6), (1, 6))
    count = 10
    even, odd = [None] * count, [None] * count
    for i in range(3):
        lo, hi = spans[i]
        sums = []
        for j in range(3):
            taps = wide_ref[i * 3 + j].reshape(3 * half, width)
            sums.append(jnp.dot(frames[lo * PITCH : hi * PITCH], taps, preferred_element_type=F32))
        at_even = down(sums[0]) + sums[1] + sums[2]
        at_odd = sums[0] + sums[1] + up(sums[2])
        for r in range(count):
            n = (r + 1) // 2 if i == 1 else r // 2
            at = slice(n * PITCH, (n + 1) * PITCH)
            even[r] = at_even[at] if even[r] is None else even[r] + at_even[at]
            odd[r] = at_odd[at] if odd[r] is None else odd[r] + at_odd[at]
    for p, rows in enumerate((even, odd)):
        for r in range(count):
            sum_ref[p, r * PITCH : (r + 1) * PITCH] = rows[r]
    step = 4 * PITCH
    size = keep_ref.shape[1]
    keep_ref[...] = sum_ref[:, pl.ds(pl.multiple_of(c * step, step), size), :]
    send_ref[...] = sum_ref[:, pl.ds(pl.multiple_of((1 - c) * step, step), size), :].astype(BF16)


def taps_of(k, acts, last_ref):
    size = 4 * PITCH
    rows = [slice(i * PITCH, i * PITCH + size) for i in range(3)]
    both = jnp.concatenate([jnp.concatenate([acts[0][at], acts[1][at]], 0) for at in rows], 1)
    parts = []
    for j in range(3):
        taps = jnp.concatenate([last_ref[k, i, j] for i in range(3)], 0)
        parts.append(jnp.dot(both, taps, preferred_element_type=F32))
    at_even = down(parts[0][size:]) + parts[1][:size] + parts[2][size:]
    at_odd = parts[0][:size] + parts[1][size:] + up(parts[2][:size])
    return jnp.concatenate([at_even, at_odd], 0)


def fine_kernel(across, place, keep_ref, got_ref, last_ref, first_ref, second_ref, mid_ref, act_ref):
    t, strip, strips = place[3], place[4], place[5]
    mid = (keep_ref[...] + got_ref[...].astype(F32)).astype(BF16)
    shape = mid.shape[1:]
    row = lax.broadcasted_iota(jnp.int32, shape, 0) // PITCH
    keep = column_mask(shape, 0, across)
    keep = keep & ((row > 0) | (strip > 0)) & ((row < 5) | (strip < strips - 1))
    acts = [jnp.where(keep, silu(mid[p].astype(F32)), 0.0).astype(BF16) for p in range(2)]
    for p in range(2):
        act_ref[p] = acts[p]
        mid_ref[p * 4 * PITCH : (p + 1) * 4 * PITCH] = mid[p, PITCH : 5 * PITCH]
    sums = [taps_of(k, acts, last_ref) for k in range(2)]
    first_ref[...] = jnp.where(t == 0, sums[0] + sums[1], sums[1]).astype(BF16)
    second_ref[...] = sums[0].astype(BF16)


def own_kernel(place, mid_ref, act_ref, last_ref, first_ref, own_ref):
    acts = [act_ref[p] for p in range(2)]
    own = mid_ref[...].astype(F32) + taps_of(2, acts, last_ref)
    late = first_ref[...].astype(F32)
    own_ref[...] = own + jnp.where(place[3] == 0, late, jnp.zeros(late.shape, F32))


def last_kernel(across, place, own_ref, first_ref, second_ref, out_ref, order_ref):
    t = place[3]
    zero = jnp.zeros(own_ref.shape, F32)
    total = (
        own_ref[...]
        + jnp.where(t >= 1, first_ref[...].astype(F32), zero)
        + jnp.where(t >= 2, second_ref[...].astype(F32), zero)
    )
    for parity in range(2):
        for h in range(4):
            at = (parity * 4 + h) * PITCH
            for half in range(2):
                order_ref[half, pl.ds(4 * parity + h, PITCH, stride=8), :] = total[
                    at : at + PITCH, 128 * half : 128 * half + 128
                ]
    for half in range(2):
        out_ref[:, 128 * half : 128 * half + 128] = order_ref[half, : 4 * across * 2].astype(BF16)


def turned(block, axis, distance):
    count = lax.axis_size(axis)
    return lax.ppermute(block, axis, [(i, (i + distance) % count) for i in range(count)])


def on_device(features, weight_one, weight_two, weight_three):
    own_block = features[0]
    height, across, shard = own_block.shape
    channels = weight_one.shape[3]
    cells = height * PITCH
    tp = ("z", "x", "c")
    kernel = jnp.transpose(weight_one, (0, 1, 2, 4, 3)).reshape(27 * shard, channels)
    small = jax.ShapeDtypeStruct((shard, cells), BF16)
    field, act_in, slices = call(
        pack_kernel,
        (small, small, jax.ShapeDtypeStruct((4, 27 * shard, channels // 4), BF16)),
        tuple(pltpu.with_memory_space_constraint(a, pltpu.HBM) for a in (jnp.transpose(own_block, (1, 2, 0)), kernel)),
        (
            pltpu.VMEM((across, shard, height), BF16),
            pltpu.VMEM((PITCH * shard, LANES), F32),
            pltpu.VMEM((cells // LANES * shard, LANES), F32),
            pltpu.SemaphoreType.DMA((5,)),
        ),
        [HBM, HBM],
    )
    frames = jnp.concatenate([act_in, turned(act_in, "tm", 1), turned(act_in, "tm", 2)], 0)
    slices = lax.all_to_all(slices, "z", 0, 0, tiled=True)
    blocks = []
    for d in range(4):
        block = turned(frames, "x", d) if d else frames
        blocks += [block, turned(block, "c", 1)]
    cut = call(
        coarse_kernel,
        jax.ShapeDtypeStruct((16, 6 * shard, LANES), BF16),
        (field, slices, *blocks),
        (
            pltpu.VMEM((3 * channels // 4, cells + 2 * LANES), BF16),
            pltpu.VMEM((12 * shard, 9 * channels // 4), BF16),
            pltpu.VMEM((4 * shard, cells + 2 * LANES), F32),
        ),
    )
    parts = lax.all_to_all(cut, ("z", "x"), 0, 0, tiled=True)
    own = pl.pallas_call(
        functools.partial(strip_kernel, across),
        out_shape=jax.ShapeDtypeStruct((6 * PITCH, channels // 2), BF16),
        scratch_shapes=[pltpu.VMEM((channels // 2, 2 * LANES), F32)],
        compiler_params=pltpu.CompilerParams(vmem_limit_bytes=LIMIT),
    )(parts)
    width = weight_two.shape[4]
    source = weight_two.reshape(3, 3, 3, -1, 2, shard, width)
    wide = call(
        stage_kernel,
        jax.ShapeDtypeStruct((9, 3, channels // 2 // shard, shard, width), BF16),
        (pltpu.with_memory_space_constraint(source, pltpu.HBM), own),
        (pltpu.SemaphoreType.DMA((9,)),),
        [HBM, pl.BlockSpec(memory_space=pl.ANY)],
    )
    rows = 6 * PITCH
    keep, send = call(
        wide_kernel,
        (jax.ShapeDtypeStruct((2, rows, width), F32), jax.ShapeDtypeStruct((2, rows, width), BF16)),
        (own, turned(own, "tm", 1), turned(own, "tm", 2), wide),
        (pltpu.VMEM((rows, 3 * channels // 2), BF16), pltpu.VMEM((2, 10 * PITCH, width), F32)),
    )
    small = jax.ShapeDtypeStruct((8 * PITCH, width), BF16)
    first, second, mid, act = call(
        functools.partial(fine_kernel, across),
        (small, small, small, jax.ShapeDtypeStruct((2, rows, width), BF16)),
        (keep, turned(send, "c", 1), weight_three),
    )
    own = call(
        own_kernel,
        jax.ShapeDtypeStruct((8 * PITCH, width), F32),
        (mid, act, weight_three, first),
    )
    decoded = call(
        functools.partial(last_kernel, across),
        jax.ShapeDtypeStruct((8 * across, width), BF16),
        (own, turned(first, "tm", 1), turned(second, "tm", 2)),
        (pltpu.VMEM((2, 8 * PITCH, 128), F32),),
    )
    return jnp.transpose(decoded.reshape(2 * across, 4, width), (1, 0, 2))[None]


def solution(mesh):
    grid = Mesh(mesh.devices.reshape(mesh.shape["tm"], 4, 4, 2), ("tm", "z", "x", "c"))
    tp = ("z", "x", "c")
    return jax.shard_map(
        on_device,
        mesh=grid,
        in_specs=(P("tm", None, None, tp), P(None, None, None, None, tp), P(), P()),
        out_specs=P("tm", tp, None, None),
        check_vma=False,
    )
```
